32 devices in a mesh: xline: 8 (over z, x), iline: 4 (over y, core).
Axes of the slice: x: 2, y: 2, z: 4, core: 2. Of those that a mesh axis runs over, the one named last changes fastest.
Arguments:
- traces: bfloat16 [16384, 1536], P(('xline', 'iline')), may hold values from -16 to 16
- trace_offset: bfloat16 [16384], P(('xline', 'iline')), may hold values from 0 to 1
- trace_owner: int32 [16384], P(('xline', 'iline')), may hold values from 0 to 31, as said below
- trace_cell: int32 [16384], P(('xline', 'iline')), may hold values from 0 to 7
- slowness: float32 [16, 16, 1536], P('xline', 'iline'), may hold values from 1 to 36
- band_start: int32 [1536], replicated, may hold values from 0 to 1528, as said below
- dip_shift: int32 [9, 16, 16], P(None, 'xline', 'iline'), may hold values from -4 to 4
Outputs:
- smoothed: float32 [16, 16, 1536], P('xline', 'iline')
The draws below stay inside these ranges and needn't reach their ends.
Inputs may be any that keep to these rules, and one draw needn't show every extreme that they name: `trace_owner`: at most 20 traces of one device (one aligned block of 512 rows) share a bin block, and one particular bin block receives exactly 20 traces from every device. band_start[t] - t lies between -(7) and 0 for every t.
All inputs are finite; a program needn't handle non-finite values.
Results may differ from the reference program's by a relative error of at most 0.0003.
Values may be sent and summed in bfloat16 or wider, within the bound.
A program may use at most 64 MiB of HBM per device.

```python
import math
import jax
import jax.numpy as jnp
from jax import lax

NT = 1536
BAND = 8
DIP = 4
TR_DEV = 512
BX = 2
BY = 4
OWNERS = 32
TRACES = 16384
NBX = 16
NBY = 16
BIN_DEV = 8
CAP = 20
N_ILINE = 4


def owner_table(key):
    base_key = jax.random.fold_in(key, 7)
    key_hot, key_popular, key_rest = jax.random.split(base_key, 3)
    hot_owner = jax.random.randint(key_hot, (), 0, OWNERS).astype(jnp.int32)
    popularity = jax.random.randint(key_popular, (OWNERS,), 0, 4) * (1 << 18)
    slot_owner = jnp.arange(OWNERS * CAP, dtype=jnp.int32) // CAP

    def one_block(block_id):
        block_key = jax.random.fold_in(key_rest, block_id)
        key_score, key_order = jax.random.split(block_key)
        scores = jax.random.randint(key_score, (OWNERS * CAP,), 0, 1 << 20) + popularity[slot_owner]
        scores = jnp.where(slot_owner == hot_owner, -1, scores)
        ranked = jnp.argsort(-scores, stable=True)
        picked = slot_owner[ranked[:TR_DEV - CAP]]
        chosen = jnp.concatenate([jnp.full((CAP,), hot_owner, jnp.int32), picked.astype(jnp.int32)])
        return jax.random.permutation(key_order, chosen)
    return jax.vmap(one_block)(jnp.arange(OWNERS)).reshape(TRACES).astype(jnp.int32)


def draw_trace_owner(key, part):
    return owner_table(key)


def draw_trace_cell(key, part):
    owner_rows = owner_table(key)
    cell_key = jax.random.fold_in(key, 11)
    key_cell, key_hole = jax.random.split(cell_key)
    cell_draw = jax.random.randint(key_cell, (TRACES,), 0, BIN_DEV)
    hole_index = jax.random.randint(key_hole, (OWNERS,), 0, 2 * BIN_DEV)
    hole_rows = hole_index[owner_rows]
    return jnp.where(cell_draw == hole_rows, (cell_draw + 1) % BIN_DEV, cell_draw).astype(jnp.int32)


def draw_band_start(key, part):
    spread = jax.random.randint(jax.random.fold_in(key, 13), (NT,), 0, BAND)
    band_begin = jnp.arange(NT, dtype=jnp.int32) + spread - BAND + 1
    return jnp.clip(band_begin, 0, NT - BAND).astype(jnp.int32)


def plant(values, stream_key, smallest, top_value):
    extent = values.shape
    index_at = [jax.random.randint(jax.random.fold_in(stream_key, axis), (), 0, extent[axis]) for axis in range(len(extent))]
    values = values.at[tuple(index_at)].set(smallest)
    longest = extent.index(max(extent))
    index_at[longest] = (index_at[longest] + 1) % extent[longest]
    return values.at[tuple(index_at)].set(top_value)


def shard_levels(own_key, extent, cuts, least, high):
    gain, own = 1.0, jax.random.fold_in(own_key, 6)
    for dim, blocks in cuts:
        steps = jnp.exp(jax.random.uniform(jax.random.fold_in(own, dim), (blocks,), jnp.float32, least / len(cuts), high / len(cuts)))
        gain = gain * jnp.repeat(steps, extent[dim] // blocks).reshape([-1 if axis == dim else 1 for axis in range(len(extent))])
    return gain


def gaussian(key, shape, scale, bound, cuts=(), kind=jnp.bfloat16):
    loudness = shard_levels(key, shape, cuts, -0.22, 0.18) if cuts else 1.0
    values = jax.random.normal(key, shape, jnp.float32) * scale * loudness
    return jnp.minimum(jnp.maximum(values, -bound), bound).astype(kind)


def setup_inputs(seed: int = 0) -> dict:
    key_list = jax.random.split(jax.random.key(seed), 8)
    return {
        "traces": gaussian(key_list[0], (TRACES, NT), 4.0, 16.0, ((0, 32),)),
        "trace_offset": jnp.clip(1.0 * jax.random.uniform(key_list[1], (TRACES,), jnp.float32) ** shard_levels(key_list[1], (TRACES,), ((0, 32),), -0.2, 0.2), 0.0, 1.0).astype(jnp.bfloat16),
        "trace_owner": draw_trace_owner(jax.random.fold_in(key_list[7], 71), 0),
        "trace_cell": draw_trace_cell(jax.random.fold_in(key_list[7], 71), 0),
        "slowness": jnp.clip(jnp.exp(math.log(36.0) - 3.583519 * jax.random.uniform(key_list[4], (NBX, NBY, NT), jnp.float32) ** shard_levels(key_list[4], (NBX, NBY, NT), ((0, 8), (1, 4)), -0.2, 0.2)), 1.0, 36.0),
        "band_start": draw_band_start(jax.random.fold_in(key_list[7], 71), 0),
        "dip_shift": plant(jax.random.randint(key_list[6], (9, NBX, NBY), -DIP, DIP + 1), jax.random.fold_in(key_list[6], 1), -DIP, DIP).astype(jnp.int32),
    }


CENTER_WEIGHT = 0.5
SIDE_WEIGHT = 0.0625

def corrected_rows(trace_rows, offset_rows, slow_rows, band_start):
    samples = trace_rows.shape[1]
    sample_times = jnp.arange(samples).astype(jnp.float32)
    moveout = jnp.sqrt(sample_times[None, :] * sample_times[None, :] + (offset_rows * offset_rows)[:, None] * slow_rows)
    numerator = jnp.zeros(moveout.shape, jnp.float32)
    denominator = jnp.zeros(moveout.shape, jnp.float32)
    for band_lag in range(BAND):
        position = band_start + band_lag
        picked = jnp.take(trace_rows, position, axis=1).astype(jnp.float32)
        distance = position.astype(jnp.float32)[None, :] - moveout
        weight = 1.0 / (1.0 + distance * distance)
        numerator = numerator + weight * picked
        denominator = denominator + weight
    return numerator / denominator

def smooth_bins(padded, dip_shift, rows_x, rows_y):
    samples = padded.shape[2]
    sample_times = jnp.arange(samples, dtype=jnp.int32)
    result = jnp.zeros((rows_x, rows_y, samples), jnp.float32)
    for neighbour in range(9):
        shift_x = neighbour // 3
        shift_y = neighbour % 3
        window = padded[shift_x:shift_x + rows_x, shift_y:shift_y + rows_y, :]
        widened = jnp.pad(window, ((0, 0), (0, 0), (DIP, DIP)))
        position = sample_times[None, None, :] + dip_shift[neighbour][:, :, None] + DIP
        shifted = jnp.take_along_axis(widened, position.astype(jnp.int32), axis=2)
        factor = CENTER_WEIGHT if neighbour == 4 else SIDE_WEIGHT
        result = result + factor * shifted
    return result

def reference(traces, trace_offset, trace_owner, trace_cell, slowness, band_start, dip_shift):
    bin_x = trace_owner // N_ILINE * BX + trace_cell // BY
    bin_y = trace_owner % N_ILINE * BY + trace_cell % BY
    bin_of = (bin_x * NBY + bin_y).astype(jnp.int32)
    slow_table = slowness.reshape(NBX * NBY, NT)

    def accumulate(running, block_parts):
        block_traces, block_offsets, block_bins = block_parts
        slow_rows = slow_table[block_bins]
        moved = corrected_rows(block_traces, block_offsets.astype(jnp.float32), slow_rows, band_start)
        return (running.at[block_bins].add(moved), None)
    blocks = (traces.reshape(OWNERS, TR_DEV, NT), trace_offset.reshape(OWNERS, TR_DEV), bin_of.reshape(OWNERS, TR_DEV))
    bin_sums, unused = lax.scan(accumulate, jnp.zeros((NBX * NBY, NT), jnp.float32), blocks)
    fold_count = jnp.zeros((NBX * NBY,), jnp.int32).at[bin_of].add(1)
    bin_stack = (bin_sums / jnp.maximum(fold_count, 1).astype(jnp.float32)[:, None]).reshape(NBX, NBY, NT)
    padded = jnp.pad(bin_stack, ((1, 1), (1, 1), (0, 0)))
    return smooth_bins(padded, dip_shift, NBX, NBY)
```

```python
import functools

import jax
import jax.numpy as jnp
from jax import lax
from jax.experimental import pallas as pl
from jax.experimental.pallas import tpu as pltpu
from jax.sharding import PartitionSpec as P

BAND = 8
DIP = 4
HALF = BAND // 2
LANES = 128
CENTER_WEIGHT = 0.5
SIDE_WEIGHT = 0.0625
MESH = pl.DeviceIdType.MESH
NT_DIMS = (((1,), (1,)), ((), ()))
f32 = jnp.float32
bf16 = jnp.bfloat16


def up_to(value, multiple):
    return -(-value // multiple) * multiple


def iota(shape, dim):
    return lax.broadcasted_iota(jnp.int32, shape, dim)


def dot(a, b):
    return jnp.dot(a, b, preferred_element_type=f32)


def parts(value, count):
    out = []
    for _ in range(count):
        piece = value.astype(bf16)
        out.append(piece)
        value = value - piece.astype(f32)
    return out


def kernel(
    c, meta_ref, traces_ref, slow_ref, band_ref, dip_ref, out_ref,
    send, send_meta, recv, recv_meta, slows, slow_parts, gather, picks, slow_rows, moved,
    sums, sums_in, stack, halo, lagged,
    s_send, s_recv, m_send, m_recv, w_send, w_recv, z_send, z_recv, h_send, h_recv,
):
    nx, nil, nz, group, cap, rows, samples = c.nx, c.nil, c.nz, c.group, c.cap, c.rows, c.samples
    ny = nil // 2
    blocks = samples // LANES
    cells = slow_ref.shape[0]
    xl = lax.axis_index("xline")
    il = lax.axis_index("iline")
    z, x = xl // nx, xl % nx
    y, core = il // 2, il % 2

    def plane(k):
        kx, ky, kc = k // nil, (k % nil) // 2, k % 2
        tx = (x + kx) % nx
        ti = ((y + ky) % ny) * 2 + (core + kc) % 2
        return tx, ti

    def plane_id(k):
        tx, ti = plane(k)
        return {"xline": z * nx + tx, "iline": ti}

    def z_id(k):
        return {"xline": ((z + k) % nz) * nx + x, "iline": il}

    around = [(dx, dy) for dx in (-1, 0, 1) for dy in (-1, 0, 1) if (dx, dy) != (0, 0)]

    def valid(dx, dy):
        ok = None
        for at, step, size in ((xl, dx, nx * nz), (il, dy, nil)):
            if step:
                here = (at + step >= 0) & (at + step < size)
                ok = here if ok is None else ok & here
        return ok

    def near_id(dx, dy):
        return {"xline": xl + dx, "iline": il + dy}

    barrier = pltpu.get_barrier_semaphore()

    def greet(target):
        pl.semaphore_signal(barrier, inc=1, device_id=target, device_id_type=MESH)

    lax.fori_loop(1, group, lambda k, _: (greet(plane_id(k)), 0)[1], 0)
    lax.fori_loop(1, nz, lambda k, _: (greet(z_id(k)), 0)[1], 0)
    for dx, dy in around:
        pl.when(valid(dx, dy))(functools.partial(lambda t: greet(t), near_id(dx, dy)))

    meta = meta_ref[...]
    owner_row, base_row = meta[0:1, :], meta[1:2, :]
    count = meta.shape[1]
    owners = up_to(group * nz, 16)
    mine = jnp.where(iota((owners, count), 0).astype(f32) == owner_row, 1.0, 0.0)
    earlier = jnp.where(iota((count, count), 0) < iota((count, count), 1), 1.0, 0.0).astype(bf16)
    before = dot(mine.astype(bf16), earlier)
    slot = base_row + jnp.sum(mine * before, axis=0, keepdims=True)
    values = jnp.concatenate([meta[2:4, :], jnp.zeros((14, count), f32)], axis=0).astype(bf16)

    def span_of(at, size):
        return 3 - jnp.where(at == 0, 1, 0) - jnp.where(at == size - 1, 1, 0)

    near = span_of(xl, nx * nz) * span_of(il, nil) - 1
    pl.semaphore_wait(barrier, (group - 1) + (nz - 1) + near)

    def slow_copy(k):
        return pltpu.make_async_remote_copy(
            src_ref=slow_ref, dst_ref=slows.at[z], send_sem=w_send.at[k], recv_sem=w_recv.at[k],
            device_id=z_id(k), device_id_type=MESH,
        )

    def row_copy(k):
        return pltpu.make_async_remote_copy(
            src_ref=send.at[k], dst_ref=recv.at[pl.ds(pl.multiple_of(k * rows, 16), rows), pl.ds(0, samples)],
            send_sem=s_send.at[k], recv_sem=s_recv.at[k], device_id=plane_id(k), device_id_type=MESH,
        )

    def meta_copy(k):
        return pltpu.make_async_remote_copy(
            src_ref=send_meta.at[k], dst_ref=recv_meta.at[k],
            send_sem=m_send.at[k], recv_sem=m_recv.at[k], device_id=plane_id(k), device_id_type=MESH,
        )

    lax.fori_loop(1, nz, lambda k, _: (slow_copy(k).start(), 0)[1], 0)

    def pack(k):
        tx, ti = plane(k)
        first = ((tx * nil + ti) * rows).astype(f32)
        hot = jnp.where(iota((c.meta_rows, count), 0).astype(f32) + first == slot, 1.0, 0.0).astype(bf16)
        chunk = dot(hot[:rows], traces_ref[...])
        chunk = pltpu.roll(chunk, LANES // 2, 1).astype(bf16)
        info = lax.dot_general(values, hot, NT_DIMS, preferred_element_type=f32).astype(bf16)
        return chunk, info

    def send_one(k, _):
        chunk, info = pack(k)
        send[k] = chunk
        send_meta[k] = info
        meta_copy(k).start()
        row_copy(k).start()
        return 0

    lax.fori_loop(1, group, send_one, 0)
    chunk, info = pack(0)
    recv[0:rows, 0:samples] = chunk
    recv_meta[0] = info

    def make_gather(b, _):
        start = pl.multiple_of(b * LANES, LANES)
        position = band_ref[:, pl.ds(start, LANES)] - start + LANES // 2
        window = iota((2 * LANES, LANES), 0)
        for pair in range(HALF):
            first = jnp.where(window == position + pair, 1.0, 0.0)
            last = jnp.where(window == position + (BAND - 1 - pair), 1.0, 0.0)
            at = pair * 2 * LANES
            gather[b, :, at : at + LANES] = (first + last).astype(bf16)
            gather[b, :, at + LANES : at + 2 * LANES] = ((first - last) * float(BAND - 1 - 2 * pair)).astype(bf16)
        return 0

    lax.fori_loop(0, blocks, make_gather, 0)

    slows[pl.ds(z, 1)] = slow_ref[...][None]
    lax.fori_loop(1, nz, lambda k, _: (slow_copy(k).wait_recv(), 0)[1], 0)
    bins = nz * cells
    table = slows[...].reshape(bins, samples)
    for i, piece in enumerate(parts(table, 3)):
        slow_parts[i * bins : (i + 1) * bins, :] = piece
    slow_parts[3 * bins :, :] = jnp.zeros((bins, samples), bf16)

    sums[...] = jnp.zeros_like(sums)
    batch = c.batch
    batch_rows = batch * rows
    tile = 32 if batch_rows % 32 == 0 else 16

    def one_batch(i, _):
        for j in range(batch):
            k = i * batch + j

            @pl.when(k > 0)
            def _():
                meta_copy(k).wait_recv()
                row_copy(k).wait_recv()

        span = pl.ds(pl.multiple_of(i * batch_rows, 16), batch_rows)
        recv[span, samples : samples + LANES] = recv[span, 0:LANES]
        same = jnp.where(iota((rows, c.meta_rows), 0) == iota((rows, c.meta_rows), 1), 1.0, 0.0).astype(bf16)
        columns = jnp.concatenate(
            [
                lax.dot_general(same, recv_meta[i * batch + j], NT_DIMS, preferred_element_type=f32)
                for j in range(batch)
            ],
            axis=0,
        )
        offset = columns[:, 0:1]
        cell = columns[:, 1:2]
        step = iota((batch_rows, 1), 0)
        base = jnp.zeros((batch_rows, 1), f32)
        for j in range(batch):
            for owner in range(1, nz):
                base = base + jnp.where((step >= j * rows + owner * cap) & (step < (j + 1) * rows), float(cells), 0.0)
        bin_id = jnp.where(cell > 0.5, base + cell - 1.0, -1.0)
        lane = iota((1, 4 * bins), 1)
        members = jnp.where((lane % bins).astype(f32) == bin_id, 1.0, 0.0).astype(bf16)
        eye = jnp.where(iota((bins, 4 * bins), 0) == iota((bins, 4 * bins), 1), 1.0, 0.0).astype(bf16)
        turned = lax.dot_general(eye, members, NT_DIMS, preferred_element_type=f32)
        fold = jnp.sum(turned, axis=1, keepdims=True)
        turned = turned.astype(bf16)
        last = pl.ds(samples, LANES)
        sums[:, :, last] = sums[:, :, last] + jnp.broadcast_to(fold, (bins, LANES)).reshape(nz, cells, LANES)
        offset2 = jnp.broadcast_to(offset * offset, (batch_rows, LANES))
        moved[2] = offset2

        def one_block(b, _):
            start = pl.multiple_of(b * LANES, LANES)
            lanes = pl.ds(start, LANES)
            picks[...] = dot(recv[span, pl.ds(start, 2 * LANES)], gather[b])
            slow_rows[...] = dot(members, slow_parts[:, lanes])
            time = (iota((1, LANES), 1) + start).astype(f32)
            time2 = time * time
            center = band_ref[:, lanes].astype(f32) + 0.5 * (BAND - 1)

            def one_tile(r, _):
                here = pl.ds(pl.multiple_of(r * tile, 16), tile)
                moveout = jnp.sqrt(time2 + moved[2, here, :] * slow_rows[here, :])
                off = center - moveout
                u = off * off
                u2 = u * u
                terms = []
                for pair in range(HALF):
                    reach = 0.5 * (BAND - 1) - pair
                    at = pair * 2 * LANES
                    v = u + (1.0 + reach * reach)
                    n = v * picks[here, at : at + LANES] + off * picks[here, at + LANES : at + 2 * LANES]
                    q = u2 + ((2.0 - 2.0 * reach * reach) * u + (1.0 + reach * reach) ** 2)
                    terms.append((n, v, q))
                while len(terms) > 1:
                    merged = []
                    for (n1, v1, q1), (n2, v2, q2) in zip(terms[::2], terms[1::2]):
                        q = None if len(terms) == 2 else q1 * q2
                        merged.append((n1 * q2 + n2 * q1, v1 * q2 + v2 * q1, q))
                    terms = merged
                n, v, _q = terms[0]
                moved[0, here, :] = n / (v + v)
                return 0

            lax.fori_loop(0, batch_rows // tile, one_tile, 0, unroll=True)
            high, low = parts(moved[0], 2)
            total = dot(turned, high) + dot(turned, low)
            sums[:, :, lanes] = sums[:, :, lanes] + total.reshape(nz, cells, LANES)
            return 0

        lax.fori_loop(0, blocks, one_block, 0)
        return 0

    lax.fori_loop(0, group // batch, one_batch, 0)

    def sum_copy(k):
        return pltpu.make_async_remote_copy(
            src_ref=sums.at[(z + k) % nz], dst_ref=sums_in.at[k - 1],
            send_sem=z_send.at[k], recv_sem=z_recv.at[k], device_id=z_id(k), device_id_type=MESH,
        )

    lax.fori_loop(1, nz, lambda k, _: (sum_copy(k).start(), 0)[1], 0)
    total = sums[pl.ds(z, 1)][0]
    for k in range(1, nz):
        sum_copy(k).wait_recv()
        total = total + sums_in[k - 1]
    stack[...] = total[:, :samples] / jnp.maximum(total[:, samples : samples + 1], 1.0)

    def halo_copy(i, dx, dy):
        return pltpu.make_async_remote_copy(
            src_ref=stack, dst_ref=halo.at[len(around) - 1 - i],
            send_sem=h_send.at[i], recv_sem=h_recv.at[len(around) - 1 - i],
            device_id=near_id(dx, dy), device_id_type=MESH,
        )

    def halo_wait(i):
        return pltpu.make_async_remote_copy(
            src_ref=stack, dst_ref=halo.at[i], send_sem=h_send.at[i], recv_sem=h_recv.at[i],
            device_id=near_id(*around[i]), device_id_type=MESH,
        )

    for i, (dx, dy) in enumerate(around):
        pl.when(valid(dx, dy))(functools.partial(lambda i, dx, dy: halo_copy(i, dx, dy).start(), i, dx, dy))

    bx, by = c.bx, c.by
    wide = by + 2
    padded_rows = (bx + 2) * wide
    lag_rows = up_to(padded_rows, 8)
    lags = 2 * DIP + 1
    lane = iota((cells, lagged.shape[0]), 1)
    place = iota((cells, 1), 0)
    weights = jnp.zeros(lane.shape, f32)
    for n in range(9):
        spot = jnp.zeros((cells, 1), jnp.int32)
        for b in range(cells):
            p = (b // by + n // 3) * wide + b % by + n % 3
            spot = jnp.where(place == b, p, spot)
        spot = spot + (dip_ref[:, n : n + 1] + DIP) * lag_rows
        weights = weights + jnp.where(lane == spot, CENTER_WEIGHT if n == 4 else SIDE_WEIGHT, 0.0)
    weights = weights.astype(bf16)
    if lagged.shape[0] > lags * lag_rows:
        lagged[lags * lag_rows :, :] = jnp.zeros((lagged.shape[0] - lags * lag_rows, samples), f32)

    for i, (dx, dy) in enumerate(around):
        ok = valid(dx, dy)
        pl.when(ok)(functools.partial(lambda i: halo_wait(i).wait_recv(), i))

        @pl.when(jnp.logical_not(ok))
        def _():
            halo[i] = jnp.zeros((cells, samples), f32)

    lines = []
    for px in range(bx + 2):
        for py in range(wide):
            dx = -1 if px == 0 else (1 if px == bx + 1 else 0)
            dy = -1 if py == 0 else (1 if py == wide - 1 else 0)
            line = (px - 1 - dx * bx) * by + (py - 1 - dy * by)
            block = stack if (dx, dy) == (0, 0) else halo.at[around.index((dx, dy))]
            lines.append(block[line : line + 1, :])
    lines += [jnp.zeros((1, samples), f32)] * (lag_rows - padded_rows)
    padded = jnp.concatenate(lines, axis=0)
    time = iota((lag_rows, samples), 1)
    for i in range(lags):
        lag = i - DIP
        shifted = padded if lag == 0 else pltpu.roll(padded, (-lag) % samples, 1)
        inside = (time + lag >= 0) & (time + lag < samples)
        lagged[i * lag_rows : (i + 1) * lag_rows, :] = jnp.where(inside, shifted, 0.0)
    result = sum(dot(weights, piece) for piece in parts(lagged[...], 3))
    for row in range(bx):
        out_ref[row] = result[row * by : (row + 1) * by, :]

    def done_plane(k, _):
        meta_copy(k).wait_send()
        row_copy(k).wait_send()
        return 0

    def done_z(k, _):
        slow_copy(k).wait_send()
        sum_copy(k).wait_send()
        return 0

    lax.fori_loop(1, group, done_plane, 0)
    lax.fori_loop(1, nz, done_z, 0)
    for i, (dx, dy) in enumerate(around):
        pl.when(valid(dx, dy))(functools.partial(lambda i, dx, dy: halo_copy(i, dx, dy).wait_send(), i, dx, dy))


class Sizes:
    pass


def body(sizes, traces, trace_offset, trace_owner, trace_cell, slowness, band_start, dip_shift):
    c = Sizes()
    size_x, c.nil = sizes
    c.nz = 1
    while c.nz * c.nz < size_x:
        c.nz *= 2
    c.nx = size_x // c.nz
    c.group = c.nx * c.nil
    count, c.samples = traces.shape
    c.cap = max(2, 5 * count // (4 * size_x * c.nil))
    c.rows = up_to(c.nz * c.cap, 16)
    c.meta_rows = up_to(c.rows, LANES)
    c.bx, c.by = slowness.shape[:2]
    c.batch = 2
    cells = c.bx * c.by
    bins = c.nz * cells
    base = (trace_owner % c.group) * c.rows + (trace_owner // c.group) * c.cap
    zero = jnp.zeros((count,), f32)
    meta = jnp.stack(
        [trace_owner.astype(f32), base.astype(f32), trace_offset.astype(f32), (trace_cell + 1).astype(f32)]
        + [zero] * 4
    )
    dips = dip_shift.reshape(9, cells).T
    samples = c.samples
    blocks = samples // LANES
    batch_rows = c.batch * c.rows
    lag_rows = up_to((c.bx + 2) * (c.by + 2), 8)
    dma = pltpu.SemaphoreType.DMA
    return pl.pallas_call(
        functools.partial(kernel, c),
        out_shape=jax.ShapeDtypeStruct((c.bx, c.by, samples), f32),
        in_specs=[pl.BlockSpec(memory_space=pltpu.VMEM)] * 5,
        out_specs=pl.BlockSpec(memory_space=pltpu.VMEM),
        scratch_shapes=[
            pltpu.VMEM((c.group, c.rows, samples), bf16),
            pltpu.VMEM((c.group, 16, c.meta_rows), bf16),
            pltpu.VMEM((c.group * c.rows, samples + LANES), bf16),
            pltpu.VMEM((c.group, 16, c.meta_rows), bf16),
            pltpu.VMEM((c.nz, cells, samples), f32),
            pltpu.VMEM((4 * bins, samples), bf16),
            pltpu.VMEM((blocks, 2 * LANES, BAND * LANES), bf16),
            pltpu.VMEM((batch_rows, BAND * LANES), f32),
            pltpu.VMEM((batch_rows, LANES), f32),
            pltpu.VMEM((3, batch_rows, LANES), f32),
            pltpu.VMEM((c.nz, cells, samples + LANES), f32),
            pltpu.VMEM((c.nz - 1, cells, samples + LANES), f32),
            pltpu.VMEM((cells, samples), f32),
            pltpu.VMEM((8, cells, samples), f32),
            pltpu.VMEM((up_to((2 * DIP + 1) * lag_rows, LANES), samples), f32),
            dma((c.group,)), dma((c.group,)), dma((c.group,)), dma((c.group,)),
            dma((c.nz,)), dma((c.nz,)), dma((c.nz,)), dma((c.nz,)),
            dma((8,)), dma((8,)),
        ],
        compiler_params=pltpu.CompilerParams(
            collective_id=0, has_side_effects=True, vmem_limit_bytes=48 * 1024 * 1024
        ),
        name="bin_stack_smooth",
    )(meta, traces, slowness.reshape(cells, samples), band_start.reshape(1, samples), dips)


def solution(mesh):
    sizes = (mesh.shape["xline"], mesh.shape["iline"])
    return jax.shard_map(
        functools.partial(body, sizes),
        mesh=mesh,
        in_specs=(
            P(("xline", "iline"), None),
            P(("xline", "iline")),
            P(("xline", "iline")),
            P(("xline", "iline")),
            P("xline", "iline", None),
            P(),
            P(None, "xline", "iline"),
        ),
        out_specs=P("xline", "iline", None),
        check_vma=False,
    )
```

```python
import functools

import jax
import jax.numpy as jnp
from jax import lax
from jax.experimental import pallas as pl
from jax.experimental.pallas import tpu as pltpu
from jax.sharding import PartitionSpec as P

BAND = 8
DIP = 4
HALF = BAND // 2
LANES = 128
CENTER_WEIGHT = 0.5
SIDE_WEIGHT = 0.0625
MESH = pl.DeviceIdType.MESH
NT_DIMS = (((1,), (1,)), ((), ()))
f32 = jnp.float32
bf16 = jnp.bfloat16


def up_to(value, multiple):
    return -(-value // multiple) * multiple


def iota(shape, dim):
    return lax.broadcasted_iota(jnp.int32, shape, dim)


def dot(a, b):
    return jnp.dot(a, b, preferred_element_type=f32)


def parts(value, count):
    out = []
    for _ in range(count):
        piece = value.astype(bf16)
        out.append(piece)
        value = value - piece.astype(f32)
    return out


def kernel(
    c, owner_ref, offset_ref, cell_ref, traces_hbm, slow_in, band_in, dip_ref, out_ref,
    traces_ref, slow_ref, band_ref, send, send_meta, recv, recv_meta, slows, slow_parts, gather, picks, slow_rows, moved,
    sums, sums_in, stack, halo, lagged,
    t_sem, s_send, s_recv, m_send, m_recv, w_send, w_recv, z_send, z_recv, h_send, h_recv,
):
    nx, nil, nz, group, cap, rows, samples = c.nx, c.nil, c.nz, c.group, c.cap, c.rows, c.samples
    ny = nil // 2
    blocks = samples // LANES
    cells = slow_ref.shape[0]
    xl = lax.axis_index("xline")
    il = lax.axis_index("iline")
    z, x = xl // nx, xl % nx
    y, core = il // 2, il % 2

    def plane(k):
        kx, ky, kc = k // nil, (k % nil) // 2, k % 2
        tx = (x + kx) % nx
        ti = ((y + ky) % ny) * 2 + (core + kc) % 2
        return tx, ti

    def plane_id(k):
        tx, ti = plane(k)
        return {"xline": z * nx + tx, "iline": ti}

    def z_id(k):
        return {"xline": ((z + k) % nz) * nx + x, "iline": il}

    around = [(dx, dy) for dx in (-1, 0, 1) for dy in (-1, 0, 1) if (dx, dy) != (0, 0)]

    def valid(dx, dy):
        ok = None
        for at, step, size in ((xl, dx, nx * nz), (il, dy, nil)):
            if step:
                here = (at + step >= 0) & (at + step < size)
                ok = here if ok is None else ok & here
        return ok

    def near_id(dx, dy):
        return {"xline": xl + dx, "iline": il + dy}

    traces_copy = pltpu.make_async_copy(traces_hbm, traces_ref, t_sem)
    traces_copy.start()

    barrier = pltpu.get_barrier_semaphore()

    def greet(target):
        pl.semaphore_signal(barrier, inc=1, device_id=target, device_id_type=MESH)

    lax.fori_loop(1, group, lambda k, _: (greet(plane_id(k)), 0)[1], 0)
    lax.fori_loop(1, nz, lambda k, _: (greet(z_id(k)), 0)[1], 0)
    for dx, dy in around:
        pl.when(valid(dx, dy))(functools.partial(lambda t: greet(t), near_id(dx, dy)))

    count = traces_ref.shape[0]
    for line in range(c.bx):
        slow_ref[line * c.by : (line + 1) * c.by, :] = slow_in[line]
    band_ref[...] = band_in[...].reshape(1, samples)
    owner_row = owner_ref[...].reshape(1, count).astype(f32)
    turn = jnp.floor((owner_row + 0.5) * (1.0 / group))
    base_row = (owner_row - turn * group) * rows + turn * cap
    offset_row = offset_ref[...].astype(f32).reshape(1, count)
    cell_row = cell_ref[...].reshape(1, count).astype(f32) + 1.0
    owners = up_to(group * nz, 16)
    mine = jnp.where(iota((owners, count), 0).astype(f32) == owner_row, 1.0, 0.0)
    earlier = jnp.where(iota((count, count), 0) < iota((count, count), 1), 1.0, 0.0).astype(bf16)
    before = dot(mine.astype(bf16), earlier)
    slot = base_row + jnp.sum(mine * before, axis=0, keepdims=True)
    values = jnp.concatenate([offset_row, cell_row, jnp.zeros((14, count), f32)], axis=0).astype(bf16)

    def span_of(at, size):
        return 3 - jnp.where(at == 0, 1, 0) - jnp.where(at == size - 1, 1, 0)

    near = span_of(xl, nx * nz) * span_of(il, nil) - 1
    pl.semaphore_wait(barrier, (group - 1) + (nz - 1) + near)

    def slow_copy(k):
        return pltpu.make_async_remote_copy(
            src_ref=slow_ref, dst_ref=slows.at[z], send_sem=w_send.at[k], recv_sem=w_recv.at[k],
            device_id=z_id(k), device_id_type=MESH,
        )

    def row_copy(k):
        return pltpu.make_async_remote_copy(
            src_ref=send.at[k], dst_ref=recv.at[pl.ds(pl.multiple_of(k * rows, 16), rows), pl.ds(0, samples)],
            send_sem=s_send.at[k], recv_sem=s_recv.at[k], device_id=plane_id(k), device_id_type=MESH,
        )

    def meta_copy(k):
        return pltpu.make_async_remote_copy(
            src_ref=send_meta.at[k], dst_ref=recv_meta.at[k],
            send_sem=m_send.at[k], recv_sem=m_recv.at[k], device_id=plane_id(k), device_id_type=MESH,
        )

    lax.fori_loop(1, nz, lambda k, _: (slow_copy(k).start(), 0)[1], 0)

    def pack(k):
        tx, ti = plane(k)
        first = ((tx * nil + ti) * rows).astype(f32)
        hot = jnp.where(iota((c.meta_rows, count), 0).astype(f32) + first == slot, 1.0, 0.0).astype(bf16)
        chunk = dot(hot[:rows], traces_ref[...])
        chunk = pltpu.roll(chunk, LANES // 2, 1).astype(bf16)
        info = lax.dot_general(values, hot, NT_DIMS, preferred_element_type=f32).astype(bf16)
        return chunk, info

    def send_one(k, _):
        chunk, info = pack(k)
        send[k] = chunk
        send_meta[k] = info
        meta_copy(k).start()
        row_copy(k).start()
        return 0

    traces_copy.wait()
    lax.fori_loop(1, group, send_one, 0)
    chunk, info = pack(0)
    recv[0:rows, 0:samples] = chunk
    recv_meta[0] = info

    def make_gather(b, _):
        start = pl.multiple_of(b * LANES, LANES)
        position = band_ref[:, pl.ds(start, LANES)] - start + LANES // 2
        window = iota((2 * LANES, LANES), 0)
        for pair in range(HALF):
            first = jnp.where(window == position + pair, 1.0, 0.0)
            last = jnp.where(window == position + (BAND - 1 - pair), 1.0, 0.0)
            at = pair * 2 * LANES
            gather[b, :, at : at + LANES] = (first + last).astype(bf16)
            gather[b, :, at + LANES : at + 2 * LANES] = ((first - last) * float(BAND - 1 - 2 * pair)).astype(bf16)
        return 0

    lax.fori_loop(0, blocks, make_gather, 0)

    slows[pl.ds(z, 1)] = slow_ref[...][None]
    lax.fori_loop(1, nz, lambda k, _: (slow_copy(k).wait_recv(), 0)[1], 0)
    bins = nz * cells
    table = slows[...].reshape(bins, samples)
    for i, piece in enumerate(parts(table, 3)):
        slow_parts[i * bins : (i + 1) * bins, :] = piece
    slow_parts[3 * bins :, :] = jnp.zeros((bins, samples), bf16)

    sums[...] = jnp.zeros_like(sums)
    batch = c.batch
    batch_rows = batch * rows
    tile = 32 if batch_rows % 32 == 0 else 16

    def one_batch(i, _):
        for j in range(batch):
            k = i * batch + j

            @pl.when(k > 0)
            def _():
                meta_copy(k).wait_recv()
                row_copy(k).wait_recv()

        span = pl.ds(pl.multiple_of(i * batch_rows, 16), batch_rows)
        recv[span, samples : samples + LANES] = recv[span, 0:LANES]
        same = jnp.where(iota((rows, c.meta_rows), 0) == iota((rows, c.meta_rows), 1), 1.0, 0.0).astype(bf16)
        columns = jnp.concatenate(
            [
                lax.dot_general(same, recv_meta[i * batch + j], NT_DIMS, preferred_element_type=f32)
                for j in range(batch)
            ],
            axis=0,
        )
        offset = columns[:, 0:1]
        cell = columns[:, 1:2]
        step = iota((batch_rows, 1), 0)
        base = jnp.zeros((batch_rows, 1), f32)
        for j in range(batch):
            for owner in range(1, nz):
                base = base + jnp.where((step >= j * rows + owner * cap) & (step < (j + 1) * rows), float(cells), 0.0)
        bin_id = jnp.where(cell > 0.5, base + cell - 1.0, -1.0)
        lane = iota((1, 4 * bins), 1)
        members = jnp.where((lane % bins).astype(f32) == bin_id, 1.0, 0.0).astype(bf16)
        eye = jnp.where(iota((bins, 4 * bins), 0) == iota((bins, 4 * bins), 1), 1.0, 0.0).astype(bf16)
        turned = lax.dot_general(eye, members, NT_DIMS, preferred_element_type=f32)
        fold = jnp.sum(turned, axis=1, keepdims=True)
        turned = turned.astype(bf16)
        last = pl.ds(samples, LANES)
        sums[:, :, last] = sums[:, :, last] + jnp.broadcast_to(fold, (bins, LANES)).reshape(nz, cells, LANES)
        offset2 = jnp.broadcast_to(offset * offset, (batch_rows, LANES))
        moved[2] = offset2

        def fetch(b, at):
            start = pl.multiple_of(b * LANES, LANES)
            picks[at] = dot(recv[span, pl.ds(start, 2 * LANES)], gather[b])
            slow_rows[at] = dot(members, slow_parts[:, pl.ds(start, LANES)])

        def one_block(b, at_slot):
            start = pl.multiple_of(b * LANES, LANES)
            lanes = pl.ds(start, LANES)
            time = (iota((1, LANES), 1) + start).astype(f32)
            time2 = time * time
            center = band_ref[:, lanes].astype(f32) + 0.5 * (BAND - 1)

            def one_tile(r, _):
                here = pl.ds(pl.multiple_of(r * tile, 16), tile)
                moveout = jnp.sqrt(time2 + moved[2, here, :] * slow_rows[at_slot, here, :])
                off = center - moveout
                u = off * off
                u2 = u * u
                terms = []
                for pair in range(HALF):
                    reach = 0.5 * (BAND - 1) - pair
                    at = pair * 2 * LANES
                    v = u + (1.0 + reach * reach)
                    n = v * picks[at_slot, here, at : at + LANES] + off * picks[at_slot, here, at + LANES : at + 2 * LANES]
                    q = u2 + ((2.0 - 2.0 * reach * reach) * u + (1.0 + reach * reach) ** 2)
                    terms.append((n, v, q))
                while len(terms) > 1:
                    merged = []
                    for (n1, v1, q1), (n2, v2, q2) in zip(terms[::2], terms[1::2]):
                        q = None if len(terms) == 2 else q1 * q2
                        merged.append((n1 * q2 + n2 * q1, v1 * q2 + v2 * q1, q))
                    terms = merged
                n, v, _q = terms[0]
                moved[at_slot, here, :] = n / (v + v)
                return 0

            lax.fori_loop(0, batch_rows // tile, one_tile, 0, unroll=True)
            high, low = parts(moved[at_slot], 2)
            total = dot(turned, high) + dot(turned, low)
            sums[:, :, lanes] = sums[:, :, lanes] + total.reshape(nz, cells, LANES)

        fetch(0, 0)

        def two_blocks(i, _):
            b = 2 * i
            fetch(b + 1, 1)
            one_block(b, 0)
            fetch((b + 2) % blocks, 0)
            one_block(b + 1, 1)
            return 0

        lax.fori_loop(0, blocks // 2, two_blocks, 0)
        return 0

    lax.fori_loop(0, group // batch, one_batch, 0)

    def sum_copy(k):
        return pltpu.make_async_remote_copy(
            src_ref=sums.at[(z + k) % nz], dst_ref=sums_in.at[k - 1],
            send_sem=z_send.at[k], recv_sem=z_recv.at[k], device_id=z_id(k), device_id_type=MESH,
        )

    lax.fori_loop(1, nz, lambda k, _: (sum_copy(k).start(), 0)[1], 0)
    total = sums[pl.ds(z, 1)][0]
    for k in range(1, nz):
        sum_copy(k).wait_recv()
        total = total + sums_in[k - 1]
    stack[...] = total[:, :samples] / jnp.maximum(total[:, samples : samples + 1], 1.0)

    def halo_copy(i, dx, dy):
        return pltpu.make_async_remote_copy(
            src_ref=stack, dst_ref=halo.at[len(around) - 1 - i],
            send_sem=h_send.at[i], recv_sem=h_recv.at[len(around) - 1 - i],
            device_id=near_id(dx, dy), device_id_type=MESH,
        )

    def halo_wait(i):
        return pltpu.make_async_remote_copy(
            src_ref=stack, dst_ref=halo.at[i], send_sem=h_send.at[i], recv_sem=h_recv.at[i],
            device_id=near_id(*around[i]), device_id_type=MESH,
        )

    for i, (dx, dy) in enumerate(around):
        pl.when(valid(dx, dy))(functools.partial(lambda i, dx, dy: halo_copy(i, dx, dy).start(), i, dx, dy))

    bx, by = c.bx, c.by
    wide = by + 2
    padded_rows = (bx + 2) * wide
    lag_rows = up_to(padded_rows, 8)
    lags = 2 * DIP + 1
    lane = iota((cells, lagged.shape[0]), 1)
    place = iota((cells, 1), 0)
    weights = jnp.zeros(lane.shape, f32)
    for n in range(9):
        for b in range(cells):
            p = (b // by + n // 3) * wide + b % by + n % 3
            spot = p + (dip_ref[b // by, b % by, n] + DIP) * lag_rows
            factor = CENTER_WEIGHT if n == 4 else SIDE_WEIGHT
            weights = weights + jnp.where((place == b) & (lane == spot), factor, 0.0)
    weights = weights.astype(bf16)
    if lagged.shape[0] > lags * lag_rows:
        lagged[lags * lag_rows :, :] = jnp.zeros((lagged.shape[0] - lags * lag_rows, samples), f32)

    for i, (dx, dy) in enumerate(around):
        ok = valid(dx, dy)
        pl.when(ok)(functools.partial(lambda i: halo_wait(i).wait_recv(), i))

        @pl.when(jnp.logical_not(ok))
        def _():
            halo[i] = jnp.zeros((cells, samples), f32)

    lines = []
    for px in range(bx + 2):
        for py in range(wide):
            dx = -1 if px == 0 else (1 if px == bx + 1 else 0)
            dy = -1 if py == 0 else (1 if py == wide - 1 else 0)
            line = (px - 1 - dx * bx) * by + (py - 1 - dy * by)
            block = stack if (dx, dy) == (0, 0) else halo.at[around.index((dx, dy))]
            lines.append(block[line : line + 1, :])
    lines += [jnp.zeros((1, samples), f32)] * (lag_rows - padded_rows)
    padded = jnp.concatenate(lines, axis=0)
    time = iota((lag_rows, samples), 1)
    for i in range(lags):
        lag = i - DIP
        shifted = padded if lag == 0 else pltpu.roll(padded, (-lag) % samples, 1)
        inside = (time + lag >= 0) & (time + lag < samples)
        lagged[i * lag_rows : (i + 1) * lag_rows, :] = jnp.where(inside, shifted, 0.0)
    result = sum(dot(weights, piece) for piece in parts(lagged[...], 3))
    for row in range(bx):
        out_ref[row] = result[row * by : (row + 1) * by, :]

    def done_plane(k, _):
        meta_copy(k).wait_send()
        row_copy(k).wait_send()
        return 0

    def done_z(k, _):
        slow_copy(k).wait_send()
        sum_copy(k).wait_send()
        return 0

    lax.fori_loop(1, group, done_plane, 0)
    lax.fori_loop(1, nz, done_z, 0)
    for i, (dx, dy) in enumerate(around):
        pl.when(valid(dx, dy))(functools.partial(lambda i, dx, dy: halo_copy(i, dx, dy).wait_send(), i, dx, dy))


class Sizes:
    pass


def body(sizes, traces, trace_offset, trace_owner, trace_cell, slowness, band_start, dip_shift):
    c = Sizes()
    size_x, c.nil = sizes
    c.nz = 1
    while c.nz * c.nz < size_x:
        c.nz *= 2
    c.nx = size_x // c.nz
    c.group = c.nx * c.nil
    count, c.samples = traces.shape
    c.cap = max(2, 5 * count // (4 * size_x * c.nil))
    c.rows = up_to(c.nz * c.cap, 16)
    c.meta_rows = up_to(c.rows, LANES)
    c.bx, c.by = slowness.shape[:2]
    c.batch = 2
    cells = c.bx * c.by
    bins = c.nz * cells
    samples = c.samples
    blocks = samples // LANES
    batch_rows = c.batch * c.rows
    lag_rows = up_to((c.bx + 2) * (c.by + 2), 8)
    dma = pltpu.SemaphoreType.DMA
    return pl.pallas_call(
        functools.partial(kernel, c),
        out_shape=jax.ShapeDtypeStruct((c.bx, c.by, samples), f32),
        in_specs=[pl.BlockSpec(memory_space=pltpu.VMEM)] * 3
        + [pl.BlockSpec(memory_space=pl.ANY)]
        + [pl.BlockSpec(memory_space=pltpu.VMEM)] * 2
        + [pl.BlockSpec(memory_space=pltpu.SMEM)],
        out_specs=pl.BlockSpec(memory_space=pltpu.VMEM),
        scratch_shapes=[
            pltpu.VMEM((count, samples), bf16),
            pltpu.VMEM((cells, samples), f32),
            pltpu.VMEM((1, samples), jnp.int32),
            pltpu.VMEM((c.group, c.rows, samples), bf16),
            pltpu.VMEM((c.group, 16, c.meta_rows), bf16),
            pltpu.VMEM((c.group * c.rows, samples + LANES), bf16),
            pltpu.VMEM((c.group, 16, c.meta_rows), bf16),
            pltpu.VMEM((c.nz, cells, samples), f32),
            pltpu.VMEM((4 * bins, samples), bf16),
            pltpu.VMEM((blocks, 2 * LANES, BAND * LANES), bf16),
            pltpu.VMEM((2, batch_rows, BAND * LANES), f32),
            pltpu.VMEM((2, batch_rows, LANES), f32),
            pltpu.VMEM((3, batch_rows, LANES), f32),
            pltpu.VMEM((c.nz, cells, samples + LANES), f32),
            pltpu.VMEM((c.nz - 1, cells, samples + LANES), f32),
            pltpu.VMEM((cells, samples), f32),
            pltpu.VMEM((8, cells, samples), f32),
            pltpu.VMEM((up_to((2 * DIP + 1) * lag_rows, LANES), samples), f32),
            dma, dma((c.group,)), dma((c.group,)), dma((c.group,)), dma((c.group,)),
            dma((c.nz,)), dma((c.nz,)), dma((c.nz,)), dma((c.nz,)),
            dma((8,)), dma((8,)),
        ],
        compiler_params=pltpu.CompilerParams(
            collective_id=0, has_side_effects=True, vmem_limit_bytes=56 * 1024 * 1024
        ),
        name="bin_stack_smooth",
    )(trace_owner, trace_offset, trace_cell, traces, slowness, band_start, dip_shift.transpose(1, 2, 0))


def solution(mesh):
    sizes = (mesh.shape["xline"], mesh.shape["iline"])
    return jax.shard_map(
        functools.partial(body, sizes),
        mesh=mesh,
        in_specs=(
            P(("xline", "iline"), None),
            P(("xline", "iline")),
            P(("xline", "iline")),
            P(("xline", "iline")),
            P("xline", "iline", None),
            P(),
            P(None, "xline", "iline"),
        ),
        out_specs=P("xline", "iline", None),
        check_vma=False,
    )
```

```python
import functools

import jax
import jax.numpy as jnp
from jax import lax
from jax.experimental import pallas as pl
from jax.experimental.pallas import tpu as pltpu
from jax.sharding import PartitionSpec as P

BAND = 8
DIP = 4
HALF = BAND // 2
LANES = 128
CENTER_WEIGHT = 0.5
SIDE_WEIGHT = 0.0625
MESH = pl.DeviceIdType.MESH
NT_DIMS = (((1,), (1,)), ((), ()))
f32 = jnp.float32
bf16 = jnp.bfloat16


def up_to(value, multiple):
    return -(-value // multiple) * multiple


def iota(shape, dim):
    return lax.broadcasted_iota(jnp.int32, shape, dim)


def dot(a, b):
    return jnp.dot(a, b, preferred_element_type=f32)


def parts(value, count):
    out = []
    for _ in range(count):
        piece = value.astype(bf16)
        out.append(piece)
        value = value - piece.astype(f32)
    return out


def kernel(
    c, owner_ref, offset_ref, cell_ref, traces_hbm, slow_in, band_in, dip_ref, out_ref,
    traces_ref, slow_ref, band_ref, send, send_meta, recv, recv_meta, slows, slow_parts, gather, picks, slow_rows, moved,
    sums, sums_in, padded, lagged,
    t_sem, s_send, s_recv, m_send, m_recv, w_send, w_recv, z_send, z_recv, h_send, h_recv,
):
    nx, nil, nz, group, cap, rows, samples = c.nx, c.nil, c.nz, c.group, c.cap, c.rows, c.samples
    ny = nil // 2
    blocks = samples // LANES
    cells = slow_ref.shape[0]
    xl = lax.axis_index("xline")
    il = lax.axis_index("iline")
    z, x = xl // nx, xl % nx
    y, core = il // 2, il % 2

    def plane(k):
        kx, ky, kc = k // nil, (k % nil) // 2, k % 2
        tx = (x + kx) % nx
        ti = ((y + ky) % ny) * 2 + (core + kc) % 2
        return tx, ti

    def plane_id(k):
        tx, ti = plane(k)
        return {"xline": z * nx + tx, "iline": ti}

    def z_id(k):
        return {"xline": ((z + k) % nz) * nx + x, "iline": il}

    around = [(dx, dy) for dx in (-1, 0, 1) for dy in (-1, 0, 1) if (dx, dy) != (0, 0)]

    def valid(dx, dy):
        ok = None
        for at, step, size in ((xl, dx, nx * nz), (il, dy, nil)):
            if step:
                here = (at + step >= 0) & (at + step < size)
                ok = here if ok is None else ok & here
        return ok

    def near_id(dx, dy):
        return {"xline": xl + dx, "iline": il + dy}

    traces_copy = pltpu.make_async_copy(traces_hbm, traces_ref, t_sem)
    traces_copy.start()

    barrier = pltpu.get_barrier_semaphore()

    def greet(target):
        pl.semaphore_signal(barrier, inc=1, device_id=target, device_id_type=MESH)

    lax.fori_loop(1, group, lambda k, _: (greet(plane_id(k)), 0)[1], 0)
    lax.fori_loop(1, nz, lambda k, _: (greet(z_id(k)), 0)[1], 0)
    for dx, dy in around:
        pl.when(valid(dx, dy))(functools.partial(lambda t: greet(t), near_id(dx, dy)))

    count = traces_ref.shape[0]
    for line in range(c.bx):
        slow_ref[line * c.by : (line + 1) * c.by, :] = slow_in[line]
    band_ref[...] = band_in[...].reshape(1, samples)
    owner_row = owner_ref[...].reshape(1, count).astype(f32)
    turn = jnp.floor((owner_row + 0.5) * (1.0 / group))
    base_row = (owner_row - turn * group) * rows + turn * cap
    offset_row = offset_ref[...].astype(f32).reshape(1, count)
    cell_row = cell_ref[...].reshape(1, count).astype(f32) + 1.0
    owners = up_to(group * nz, 16)
    mine = jnp.where(iota((owners, count), 0).astype(f32) == owner_row, 1.0, 0.0)
    earlier = jnp.where(iota((count, count), 0) < iota((count, count), 1), 1.0, 0.0).astype(bf16)
    before = dot(mine.astype(bf16), earlier)
    slot = base_row + jnp.sum(mine * before, axis=0, keepdims=True)
    values = jnp.concatenate([offset_row, cell_row, jnp.zeros((14, count), f32)], axis=0).astype(bf16)

    def span_of(at, size):
        return 3 - jnp.where(at == 0, 1, 0) - jnp.where(at == size - 1, 1, 0)

    near = span_of(xl, nx * nz) * span_of(il, nil) - 1
    pl.semaphore_wait(barrier, (group - 1) + (nz - 1) + near)

    def slow_copy(k):
        return pltpu.make_async_remote_copy(
            src_ref=slow_ref, dst_ref=slows.at[z], send_sem=w_send.at[k], recv_sem=w_recv.at[k],
            device_id=z_id(k), device_id_type=MESH,
        )

    def row_copy(k):
        return pltpu.make_async_remote_copy(
            src_ref=send.at[k], dst_ref=recv.at[pl.ds(pl.multiple_of(k * rows, 16), rows), pl.ds(0, samples)],
            send_sem=s_send.at[k], recv_sem=s_recv.at[k], device_id=plane_id(k), device_id_type=MESH,
        )

    def meta_copy(k):
        return pltpu.make_async_remote_copy(
            src_ref=send_meta.at[k], dst_ref=recv_meta.at[k],
            send_sem=m_send.at[k], recv_sem=m_recv.at[k], device_id=plane_id(k), device_id_type=MESH,
        )

    lax.fori_loop(1, nz, lambda k, _: (slow_copy(k).start(), 0)[1], 0)

    def pack(k):
        tx, ti = plane(k)
        first = ((tx * nil + ti) * rows).astype(f32)
        hot = jnp.where(iota((c.meta_rows, count), 0).astype(f32) + first == slot, 1.0, 0.0).astype(bf16)
        chunk = dot(hot[:rows], traces_ref[...])
        chunk = pltpu.roll(chunk, LANES // 2, 1).astype(bf16)
        info = lax.dot_general(values, hot, NT_DIMS, preferred_element_type=f32).astype(bf16)
        return chunk, info

    def send_one(k, _):
        chunk, info = pack(k)
        send[k] = chunk
        send_meta[k] = info
        meta_copy(k).start()
        row_copy(k).start()
        return 0

    traces_copy.wait()
    lax.fori_loop(1, group, send_one, 0)
    chunk, info = pack(0)
    recv[0:rows, 0:samples] = chunk
    recv_meta[0] = info

    def make_gather(b, _):
        start = pl.multiple_of(b * LANES, LANES)
        position = band_ref[:, pl.ds(start, LANES)] - start + LANES // 2
        window = iota((2 * LANES, LANES), 0)
        for pair in range(HALF):
            first = jnp.where(window == position + pair, 1.0, 0.0)
            last = jnp.where(window == position + (BAND - 1 - pair), 1.0, 0.0)
            at = pair * 2 * LANES
            gather[b, :, at : at + LANES] = (first + last).astype(bf16)
            gather[b, :, at + LANES : at + 2 * LANES] = ((first - last) * float(BAND - 1 - 2 * pair)).astype(bf16)
        return 0

    lax.fori_loop(0, blocks, make_gather, 0)

    slows[pl.ds(z, 1)] = slow_ref[...][None]
    lax.fori_loop(1, nz, lambda k, _: (slow_copy(k).wait_recv(), 0)[1], 0)
    bins = nz * cells
    table = slows[...].reshape(bins, samples)
    for i, piece in enumerate(parts(table, 3)):
        slow_parts[i * bins : (i + 1) * bins, :] = piece
    slow_parts[3 * bins :, :] = jnp.zeros((bins, samples), bf16)

    sums[...] = jnp.zeros_like(sums)
    batch = c.batch
    batch_rows = batch * rows
    tile = 32 if batch_rows % 32 == 0 else 16

    pieces = c.pieces
    per_piece = blocks // pieces

    def piece_lanes(p):
        first = 0 if p == 0 else LANES + p * per_piece * LANES
        return pl.ds(first, LANES + (p + 1) * per_piece * LANES - first)

    def sum_copy(k, p):
        return pltpu.make_async_remote_copy(
            src_ref=sums.at[(z + k) % nz, :, piece_lanes(p)], dst_ref=sums_in.at[k - 1, :, piece_lanes(p)],
            send_sem=z_send.at[k * pieces + p], recv_sem=z_recv.at[k * pieces + p],
            device_id=z_id(k), device_id_type=MESH,
        )

    def one_batch(i, last):
        for j in range(batch):
            k = i * batch + j

            @pl.when(k > 0)
            def _():
                meta_copy(k).wait_recv()
                row_copy(k).wait_recv()

        span = pl.ds(pl.multiple_of(i * batch_rows, 16), batch_rows)
        recv[span, samples : samples + LANES] = recv[span, 0:LANES]
        same = jnp.where(iota((rows, c.meta_rows), 0) == iota((rows, c.meta_rows), 1), 1.0, 0.0).astype(bf16)
        columns = jnp.concatenate(
            [
                lax.dot_general(same, recv_meta[i * batch + j], NT_DIMS, preferred_element_type=f32)
                for j in range(batch)
            ],
            axis=0,
        )
        offset = columns[:, 0:1]
        cell = columns[:, 1:2]
        step = iota((batch_rows, 1), 0)
        base = jnp.zeros((batch_rows, 1), f32)
        for j in range(batch):
            for owner in range(1, nz):
                base = base + jnp.where((step >= j * rows + owner * cap) & (step < (j + 1) * rows), float(cells), 0.0)
        bin_id = jnp.where(cell > 0.5, base + cell - 1.0, -1.0)
        lane = iota((1, 4 * bins), 1)
        members = jnp.where((lane % bins).astype(f32) == bin_id, 1.0, 0.0).astype(bf16)
        eye = jnp.where(iota((bins, 4 * bins), 0) == iota((bins, 4 * bins), 1), 1.0, 0.0).astype(bf16)
        turned = lax.dot_general(eye, members, NT_DIMS, preferred_element_type=f32)
        fold = jnp.sum(turned, axis=1, keepdims=True)
        turned = turned.astype(bf16)
        head = pl.ds(0, LANES)
        sums[:, :, head] = sums[:, :, head] + jnp.broadcast_to(fold, (bins, LANES)).reshape(nz, cells, LANES)
        offset2 = jnp.broadcast_to(offset * offset, (batch_rows, LANES))
        moved[2] = offset2

        def fetch(b, at):
            start = pl.multiple_of(b * LANES, LANES)
            picks[at] = dot(recv[span, pl.ds(start, 2 * LANES)], gather[b])
            slow_rows[at] = dot(members, slow_parts[:, pl.ds(start, LANES)])

        def one_block(b, at_slot):
            start = pl.multiple_of(b * LANES, LANES)
            lanes = pl.ds(start, LANES)
            time = (iota((1, LANES), 1) + start).astype(f32)
            time2 = time * time
            center = band_ref[:, lanes].astype(f32) + 0.5 * (BAND - 1) - time

            def one_tile(r, _):
                here = pl.ds(pl.multiple_of(r * tile, 16), tile)
                delay2 = moved[2, here, :] * slow_rows[at_slot, here, :]
                square = jnp.maximum(time2 + delay2, 1e-30)
                off = center - delay2 * pl.reciprocal(time + square * lax.rsqrt(square), approx=True)
                u = off * off
                u2 = u * u
                terms = []
                for pair in range(HALF):
                    reach = 0.5 * (BAND - 1) - pair
                    at = pair * 2 * LANES
                    v = u + (1.0 + reach * reach)
                    n = v * picks[at_slot, here, at : at + LANES] + off * picks[at_slot, here, at + LANES : at + 2 * LANES]
                    q = u2 + ((2.0 - 2.0 * reach * reach) * u + (1.0 + reach * reach) ** 2)
                    terms.append((n, v, q))
                while len(terms) > 1:
                    merged = []
                    for (n1, v1, q1), (n2, v2, q2) in zip(terms[::2], terms[1::2]):
                        q = None if len(terms) == 2 else q1 * q2
                        merged.append((n1 * q2 + n2 * q1, v1 * q2 + v2 * q1, q))
                    terms = merged
                n, v, _q = terms[0]
                v = v + v
                inverse = pl.reciprocal(v, approx=True)
                moved[at_slot, here, :] = n * (inverse * (2.0 - v * inverse))
                return 0

            lax.fori_loop(0, batch_rows // tile, one_tile, 0, unroll=True)
            high, low = parts(moved[at_slot], 2)
            total = dot(turned, high) + dot(turned, low)
            after = pl.ds(pl.multiple_of(start + LANES, LANES), LANES)
            sums[:, :, after] = sums[:, :, after] + total.reshape(nz, cells, LANES)

        fetch(0, 0)

        def two_blocks(i, _):
            b = 2 * i
            fetch(b + 1, 1)
            one_block(b, 0)
            fetch((b + 2) % blocks, 0)
            one_block(b + 1, 1)
            return 0

        if not last:
            lax.fori_loop(0, blocks // 2, two_blocks, 0)
            return 0
        for p in range(pieces):
            lax.fori_loop(p * per_piece // 2, (p + 1) * per_piece // 2, two_blocks, 0)
            for k in range(1, nz):
                sum_copy(k, p).start()

    lax.fori_loop(0, group // batch - 1, lambda i, _: one_batch(i, False), 0)
    one_batch(group // batch - 1, True)

    bx, by = c.bx, c.by
    wide = by + 2

    def strips(dx, dy):
        rows_x = range(bx) if dx == 0 else [bx - 1 if dx == 1 else 0]
        row_y, run = (0, by) if dy == 0 else (by - 1 if dy == 1 else 0, 1)
        return [
            ((row + 1) * wide + row_y + 1, (row + 1 - dx * bx) * wide + row_y + 1 - dy * by, run) for row in rows_x
        ]

    strip_list = [(dx, dy) + strip for dx, dy in around for strip in strips(dx, dy)]

    def halo_copy(j, p, way=1):
        dx, dy, source, target, run = strip_list[j]
        lanes = pl.ds(p * per_piece * LANES, per_piece * LANES)
        return pltpu.make_async_remote_copy(
            src_ref=padded.at[pl.ds(source, run), :, lanes], dst_ref=padded.at[pl.ds(target, run), :, lanes],
            send_sem=h_send.at[j * pieces + p], recv_sem=h_recv.at[j * pieces + p],
            device_id=near_id(way * dx, way * dy), device_id_type=MESH,
        )

    fold = None
    for p in range(pieces):
        total = sums[pl.ds(z, 1), :, piece_lanes(p)][0]
        for k in range(1, nz):
            sum_copy(k, p).wait_recv()
            total = total + sums_in[k - 1, :, piece_lanes(p)]
        if p == 0:
            fold = jnp.maximum(total[:, :1], 1.0)
            total = total[:, LANES:]
        total = total / fold
        for b in range(cells):
            padded[(b // by + 1) * wide + b % by + 1, :, p * per_piece * LANES : (p + 1) * per_piece * LANES] = total[b : b + 1]
        for dx, dy in around:

            @pl.when(valid(dx, dy))
            def _():
                for j, strip in enumerate(strip_list):
                    if strip[:2] == (dx, dy):
                        halo_copy(j, p).start()

    padded_rows = (bx + 2) * wide
    lag_rows = up_to(padded_rows, 8)
    lags = 2 * DIP + 1
    lane = iota((cells, lagged.shape[0]), 1)
    place = iota((cells, 1), 0)
    weights = jnp.zeros(lane.shape, f32)
    for n in range(9):
        for b in range(cells):
            p = (b // by + n // 3) * wide + b % by + n % 3
            spot = p + (dip_ref[b // by, b % by, n] + DIP) * lag_rows
            factor = CENTER_WEIGHT if n == 4 else SIDE_WEIGHT
            weights = weights + jnp.where((place == b) & (lane == spot), factor, 0.0)
    weights = weights.astype(bf16)
    if lagged.shape[0] > lags * lag_rows:
        lagged[lags * lag_rows :, :] = jnp.zeros((lagged.shape[0] - lags * lag_rows, samples), f32)

    for dx, dy in around:
        ok = valid(-dx, -dy)
        mine_in = [j for j, strip in enumerate(strip_list) if strip[:2] == (dx, dy)]

        @pl.when(ok)
        def _():
            for j in mine_in:
                for p in range(pieces):
                    halo_copy(j, p, -1).wait_recv()

        @pl.when(jnp.logical_not(ok))
        def _():
            for j in mine_in:
                target, run = strip_list[j][3:]
                padded[pl.ds(target, run)] = jnp.zeros((run, 1, samples), f32)

    lines = [padded[line] for line in range(padded_rows)]
    lines += [jnp.zeros((1, samples), f32)] * (lag_rows - padded_rows)
    whole = jnp.concatenate(lines, axis=0)
    time = iota((lag_rows, samples), 1)
    for i in range(lags):
        lag = i - DIP
        shifted = whole if lag == 0 else pltpu.roll(whole, (-lag) % samples, 1)
        inside = (time + lag >= 0) & (time + lag < samples)
        lagged[i * lag_rows : (i + 1) * lag_rows, :] = jnp.where(inside, shifted, 0.0)
    result = sum(dot(weights, piece) for piece in parts(lagged[...], 3))
    for row in range(bx):
        out_ref[row] = result[row * by : (row + 1) * by, :]

    def done_plane(k, _):
        meta_copy(k).wait_send()
        row_copy(k).wait_send()
        return 0

    def done_z(k, _):
        slow_copy(k).wait_send()
        for p in range(pieces):
            sum_copy(k, p).wait_send()
        return 0

    lax.fori_loop(1, group, done_plane, 0)
    lax.fori_loop(1, nz, done_z, 0)
    for dx, dy in around:

        @pl.when(valid(dx, dy))
        def _():
            for j, strip in enumerate(strip_list):
                if strip[:2] == (dx, dy):
                    for p in range(pieces):
                        halo_copy(j, p).wait_send()


class Sizes:
    pass


def body(sizes, traces, trace_offset, trace_owner, trace_cell, slowness, band_start, dip_shift):
    c = Sizes()
    size_x, c.nil = sizes
    c.nz = 1
    while c.nz * c.nz < size_x:
        c.nz *= 2
    c.nx = size_x // c.nz
    c.group = c.nx * c.nil
    count, c.samples = traces.shape
    c.cap = max(2, 5 * count // (4 * size_x * c.nil))
    c.rows = up_to(c.nz * c.cap, 16)
    c.meta_rows = up_to(c.rows, LANES)
    c.bx, c.by = slowness.shape[:2]
    c.batch = 2
    c.pieces = 3
    cells = c.bx * c.by
    bins = c.nz * cells
    samples = c.samples
    blocks = samples // LANES
    batch_rows = c.batch * c.rows
    lag_rows = up_to((c.bx + 2) * (c.by + 2), 8)
    dma = pltpu.SemaphoreType.DMA
    strip_count = 2 + 2 * c.bx + 4
    return pl.pallas_call(
        functools.partial(kernel, c),
        out_shape=jax.ShapeDtypeStruct((c.bx, c.by, samples), f32),
        in_specs=[pl.BlockSpec(memory_space=pltpu.VMEM)] * 3
        + [pl.BlockSpec(memory_space=pl.ANY)]
        + [pl.BlockSpec(memory_space=pltpu.VMEM)] * 2
        + [pl.BlockSpec(memory_space=pltpu.SMEM)],
        out_specs=pl.BlockSpec(memory_space=pltpu.VMEM),
        scratch_shapes=[
            pltpu.VMEM((count, samples), bf16),
            pltpu.VMEM((cells, samples), f32),
            pltpu.VMEM((1, samples), jnp.int32),
            pltpu.VMEM((c.group, c.rows, samples), bf16),
            pltpu.VMEM((c.group, 16, c.meta_rows), bf16),
            pltpu.VMEM((c.group * c.rows, samples + LANES), bf16),
            pltpu.VMEM((c.group, 16, c.meta_rows), bf16),
            pltpu.VMEM((c.nz, cells, samples), f32),
            pltpu.VMEM((4 * bins, samples), bf16),
            pltpu.VMEM((blocks, 2 * LANES, BAND * LANES), bf16),
            pltpu.VMEM((2, batch_rows, BAND * LANES), f32),
            pltpu.VMEM((2, batch_rows, LANES), f32),
            pltpu.VMEM((3, batch_rows, LANES), f32),
            pltpu.VMEM((c.nz, cells, samples + LANES), f32),
            pltpu.VMEM((c.nz - 1, cells, samples + LANES), f32),
            pltpu.VMEM(((c.bx + 2) * (c.by + 2), 1, samples), f32),
            pltpu.VMEM((up_to((2 * DIP + 1) * lag_rows, LANES), samples), f32),
            dma, dma((c.group,)), dma((c.group,)), dma((c.group,)), dma((c.group,)),
            dma((c.nz,)), dma((c.nz,)), dma((c.nz * c.pieces,)), dma((c.nz * c.pieces,)),
            dma((strip_count * c.pieces,)), dma((strip_count * c.pieces,)),
        ],
        compiler_params=pltpu.CompilerParams(
            collective_id=0, has_side_effects=True, vmem_limit_bytes=56 * 1024 * 1024
        ),
        name="bin_stack_smooth",
    )(trace_owner, trace_offset, trace_cell, traces, slowness, band_start, dip_shift.transpose(1, 2, 0))


def solution(mesh):
    sizes = (mesh.shape["xline"], mesh.shape["iline"])
    return jax.shard_map(
        functools.partial(body, sizes),
        mesh=mesh,
        in_specs=(
            P(("xline", "iline"), None),
            P(("xline", "iline")),
            P(("xline", "iline")),
            P(("xline", "iline")),
            P("xline", "iline", None),
            P(),
            P(None, "xline", "iline"),
        ),
        out_specs=P("xline", "iline", None),
        check_vma=False,
    )
```

```python
import functools

import jax
import jax.numpy as jnp
from jax import lax
from jax.experimental import pallas as pl
from jax.experimental.pallas import tpu as pltpu
from jax.sharding import PartitionSpec as P

BAND = 8
DIP = 4
HALF = BAND // 2
LANES = 128
CENTER_WEIGHT = 0.5
SIDE_WEIGHT = 0.0625
MESH = pl.DeviceIdType.MESH
NT_DIMS = (((1,), (1,)), ((), ()))
f32 = jnp.float32
bf16 = jnp.bfloat16


def up_to(value, multiple):
    return -(-value // multiple) * multiple


def iota(shape, dim):
    return lax.broadcasted_iota(jnp.int32, shape, dim)


def dot(a, b):
    return jnp.dot(a, b, preferred_element_type=f32)


def parts(value, count):
    out = []
    for _ in range(count):
        piece = value.astype(bf16)
        out.append(piece)
        value = value - piece.astype(f32)
    return out


def kernel(
    c, owner_ref, offset_ref, cell_ref, traces_hbm, slow_in, band_in, dip_ref, out_ref,
    traces_ref, slow_ref, band_ref, send, send_meta, recv, recv_meta, slows, slow_parts, gather, picks, slow_rows, moved,
    sums, sums_in, padded, lagged,
    t_sem, s_send, s_recv, m_send, m_recv, w_send, w_recv, z_send, z_recv, h_send, h_recv,
):
    nx, nil, nz, group, cap, rows, samples = c.nx, c.nil, c.nz, c.group, c.cap, c.rows, c.samples
    ny = nil // 2
    ring = c.ring
    half = samples // 2
    cols = half + LANES
    half_blocks = half // LANES
    blocks = samples // LANES
    cells = slow_ref.shape[0]
    xl = lax.axis_index("xline")
    il = lax.axis_index("iline")
    z, x = xl // nx, xl % nx
    y, core = il // 2, il % 2

    def plane(h, k):
        tx = (x + (1 - h) * (k // 2)) % nx
        ty = (y + h * (k // 2)) % ny
        return tx, ty, (core + k % 2) % 2

    def plane_id(h, k):
        tx, ty, tc = plane(h, k)
        return {"xline": z * nx + tx, "iline": ty * 2 + tc}

    def column(h, k):
        tz = (z + k // nx) % nz
        tx = (x + h * (k % nx)) % nx
        ty = (y + (1 - h) * (k % nx)) % ny
        return tz, tx, ty

    def column_id(h, k):
        tz, tx, ty = column(h, k)
        return {"xline": tz * nx + tx, "iline": ty * 2 + core}

    def place_of(h, k):
        tz, tx, ty = column(h, k)
        return tz * nx + (1 - h) * ty + h * tx

    around = [(dx, dy) for dx in (-1, 0, 1) for dy in (-1, 0, 1) if (dx, dy) != (0, 0)]

    def valid(dx, dy):
        ok = None
        for at, step, size in ((xl, dx, nx * nz), (il, dy, nil)):
            if step:
                here = (at + step >= 0) & (at + step < size)
                ok = here if ok is None else ok & here
        return ok

    def near_id(dx, dy):
        return {"xline": xl + dx, "iline": il + dy}

    traces_copy = pltpu.make_async_copy(traces_hbm, traces_ref, t_sem)
    traces_copy.start()

    barrier = pltpu.get_barrier_semaphore()

    def greet(target):
        pl.semaphore_signal(barrier, inc=1, device_id=target, device_id_type=MESH)

    for h in range(2):
        lax.fori_loop(1, group, lambda k, _: (greet(plane_id(h, k)), 0)[1], 0)
        lax.fori_loop(1, ring, lambda k, _: (greet(column_id(h, k)), 0)[1], 0)
    for dx, dy in around:
        pl.when(valid(dx, dy))(functools.partial(lambda t: greet(t), near_id(dx, dy)))

    count = traces_ref.shape[0]
    for line in range(c.bx):
        slow_ref[line * c.by : (line + 1) * c.by, :] = slow_in[line]
    band_ref[...] = band_in[...].reshape(1, samples)
    owner_row = owner_ref[...].reshape(1, count).astype(f32)

    def split(value, size):
        quotient = jnp.floor((value + 0.5) * (1.0 / size))
        return quotient, value - quotient * size

    owner_xl, owner_il = split(owner_row, nil)
    owner_z, owner_x = split(owner_xl, nx)
    owner_y, owner_core = split(owner_il, 2)
    bases = [
        (owner_x * 2.0 + owner_core) * rows + (owner_z * nx + owner_y) * cap,
        (owner_y * 2.0 + owner_core) * rows + (owner_z * nx + owner_x) * cap,
    ]
    offset_row = offset_ref[...].astype(f32).reshape(1, count)
    cell_row = cell_ref[...].reshape(1, count).astype(f32) + 1.0
    owners = up_to(group * ring, 16)
    mine = jnp.where(iota((owners, count), 0).astype(f32) == owner_row, 1.0, 0.0)
    earlier = jnp.where(iota((count, count), 0) < iota((count, count), 1), 1.0, 0.0).astype(bf16)
    before = dot(mine.astype(bf16), earlier)
    rank = jnp.sum(mine * before, axis=0, keepdims=True)
    slots = [base + rank for base in bases]
    values = jnp.concatenate([offset_row, cell_row, jnp.zeros((14, count), f32)], axis=0).astype(bf16)

    def span_of(at, size):
        return 3 - jnp.where(at == 0, 1, 0) - jnp.where(at == size - 1, 1, 0)

    near = span_of(xl, nx * nz) * span_of(il, nil) - 1
    pl.semaphore_wait(barrier, 2 * (group - 1) + 2 * (ring - 1) + near)

    def slow_copy(h, k):
        return pltpu.make_async_remote_copy(
            src_ref=slow_ref.at[:, pl.ds(h * half, half)], dst_ref=slows.at[h, place_of(h, 0)],
            send_sem=w_send.at[h * ring + k], recv_sem=w_recv.at[h * ring + k],
            device_id=column_id(h, k), device_id_type=MESH,
        )

    def row_copy(h, k):
        n = h * group + k
        return pltpu.make_async_remote_copy(
            src_ref=send.at[n], dst_ref=recv.at[pl.ds(pl.multiple_of(n * rows, 16), rows)],
            send_sem=s_send.at[n], recv_sem=s_recv.at[n], device_id=plane_id(h, k), device_id_type=MESH,
        )

    def meta_copy(h, k):
        n = h * group + k
        return pltpu.make_async_remote_copy(
            src_ref=send_meta.at[n], dst_ref=recv_meta.at[n],
            send_sem=m_send.at[n], recv_sem=m_recv.at[n], device_id=plane_id(h, k), device_id_type=MESH,
        )

    for h in range(2):
        lax.fori_loop(1, ring, lambda k, _: (slow_copy(h, k).start(), 0)[1], 0)

    def pack(h, k):
        tx, ty, tc = plane(h, k)
        first = (((ty if h else tx) * 2 + tc) * rows).astype(f32)
        hot = jnp.where(iota((c.meta_rows, count), 0).astype(f32) + first == slots[h], 1.0, 0.0).astype(bf16)
        start = h * (samples - cols)
        chunk = dot(hot[:rows], traces_ref[:, start : start + cols])
        chunk = pltpu.roll(chunk, cols - LANES // 2 if h else LANES // 2, 1).astype(bf16)
        info = lax.dot_general(values, hot, NT_DIMS, preferred_element_type=f32).astype(bf16)
        return chunk, info

    def send_one(j, _):
        k = j % (group - 1) + 1
        for h in range(2):
            chunk, info = pack(h, k)
            send[h * group + k] = chunk
            send_meta[h * group + k] = info
            meta_copy(h, k).start()
            row_copy(h, k).start()
        return 0

    traces_copy.wait()
    lax.fori_loop(1, group, send_one, 0)
    for h in range(2):
        chunk, info = pack(h, 0)
        recv[h * group * rows : (h * group + 1) * rows, :] = chunk
        recv_meta[h * group] = info

    def make_gather(b, _):
        start = pl.multiple_of(b * LANES, LANES)
        position = band_ref[:, pl.ds(start, LANES)] - start + LANES // 2
        window = iota((2 * LANES, LANES), 0)
        for pair in range(HALF):
            first = jnp.where(window == position + pair, 1.0, 0.0)
            last = jnp.where(window == position + (BAND - 1 - pair), 1.0, 0.0)
            at = pair * 2 * LANES
            gather[b, :, at : at + LANES] = (first + last).astype(bf16)
            gather[b, :, at + LANES : at + 2 * LANES] = ((first - last) * float(BAND - 1 - 2 * pair)).astype(bf16)
        return 0

    lax.fori_loop(0, blocks, make_gather, 0)

    bins = ring * cells
    for h in range(2):
        slows[h, pl.ds(place_of(h, 0), 1)] = slow_ref[:, h * half : (h + 1) * half][None]
        lax.fori_loop(1, ring, lambda k, _: (slow_copy(h, k).wait_recv(), 0)[1], 0)
        table = slows[h].reshape(bins, half)
        for i, piece in enumerate(parts(table, 3)):
            slow_parts[h, i * bins : (i + 1) * bins, :] = piece
        slow_parts[h, 3 * bins :, :] = jnp.zeros((bins, half), bf16)

    sums[...] = jnp.zeros_like(sums)
    tile = 32 if rows % 32 == 0 else 16
    counts = c.counts

    def piece_lanes(h, p):
        per_piece = half_blocks // counts[h]
        first = 0 if p == 0 else LANES + p * per_piece * LANES
        return pl.ds(first, LANES + (p + 1) * per_piece * LANES - first)

    def piece_id(h, p):
        return h * counts[0] + p

    pieces = sum(counts)
    piece_list = [(h, p) for h in range(2) for p in range(counts[h])]

    def sum_copy(h, p, k):
        n = piece_id(h, p) * ring + k
        return pltpu.make_async_remote_copy(
            src_ref=sums.at[h, place_of(h, k), :, piece_lanes(h, p)], dst_ref=sums_in.at[h, k - 1, :, piece_lanes(h, p)],
            send_sem=z_send.at[n], recv_sem=z_recv.at[n],
            device_id=column_id(h, k), device_id_type=MESH,
        )

    def send_sums(h, p):
        lax.fori_loop(1, ring, lambda k, _: (sum_copy(h, p, k).start(), 0)[1], 0)

    def one_batch(h, k, last):
        n = h * group + k

        @pl.when(k > 0)
        def _():
            meta_copy(h, k).wait_recv()
            row_copy(h, k).wait_recv()

        span = pl.ds(pl.multiple_of(n * rows, 16), rows)
        batch_rows = rows
        same = jnp.where(iota((rows, c.meta_rows), 0) == iota((rows, c.meta_rows), 1), 1.0, 0.0).astype(bf16)
        columns = lax.dot_general(same, recv_meta[n], NT_DIMS, preferred_element_type=f32)
        offset = columns[:, 0:1]
        cell = columns[:, 1:2]
        step = iota((batch_rows, 1), 0)
        base = jnp.zeros((batch_rows, 1), f32)
        for owner in range(1, ring):
            base = base + jnp.where(step >= owner * cap, float(cells), 0.0)
        bin_id = jnp.where(cell > 0.5, base + cell - 1.0, -1.0)
        lane = iota((1, 4 * bins), 1)
        members = jnp.where((lane % bins).astype(f32) == bin_id, 1.0, 0.0).astype(bf16)
        eye = jnp.where(iota((bins, 4 * bins), 0) == iota((bins, 4 * bins), 1), 1.0, 0.0).astype(bf16)
        turned = lax.dot_general(eye, members, NT_DIMS, preferred_element_type=f32)
        fold = jnp.sum(turned, axis=1, keepdims=True)
        turned = turned.astype(bf16)
        head = pl.ds(0, LANES)
        sums[h, :, :, head] = sums[h, :, :, head] + jnp.broadcast_to(fold, (bins, LANES)).reshape(ring, cells, LANES)
        offset2 = jnp.broadcast_to(offset * offset, (batch_rows, LANES))
        moved[2] = offset2

        def fetch(b, at):
            start = pl.multiple_of(b * LANES, LANES)
            picks[at] = dot(recv[span, pl.ds(start, 2 * LANES)], gather[h * half_blocks + b])
            slow_rows[at] = dot(members, slow_parts[h, :, pl.ds(start, LANES)])

        def one_block(b, at_slot):
            start = pl.multiple_of(b * LANES, LANES)
            here_start = pl.multiple_of(start + h * half, LANES)
            lanes = pl.ds(here_start, LANES)
            time = (iota((1, LANES), 1) + here_start).astype(f32)
            time2 = time * time
            center = band_ref[:, lanes].astype(f32) + 0.5 * (BAND - 1) - time

            def one_tile(r, _):
                here = pl.ds(pl.multiple_of(r * tile, 16), tile)
                delay2 = moved[2, here, :] * slow_rows[at_slot, here, :]
                square = jnp.maximum(time2 + delay2, 1e-30)
                off = center - delay2 * pl.reciprocal(time + square * lax.rsqrt(square), approx=True)
                u = off * off
                u2 = u * u
                terms = []
                for pair in range(HALF):
                    reach = 0.5 * (BAND - 1) - pair
                    at = pair * 2 * LANES
                    v = u + (1.0 + reach * reach)
                    n = v * picks[at_slot, here, at : at + LANES] + off * picks[at_slot, here, at + LANES : at + 2 * LANES]
                    q = u2 + ((2.0 - 2.0 * reach * reach) * u + (1.0 + reach * reach) ** 2)
                    terms.append((n, v, q))
                while len(terms) > 1:
                    merged = []
                    for (n1, v1, q1), (n2, v2, q2) in zip(terms[::2], terms[1::2]):
                        q = None if len(terms) == 2 else q1 * q2
                        merged.append((n1 * q2 + n2 * q1, v1 * q2 + v2 * q1, q))
                    terms = merged
                n, v, _q = terms[0]
                v = v + v
                inverse = pl.reciprocal(v, approx=True)
                moved[at_slot, here, :] = n * (inverse * (2.0 - v * inverse))
                return 0

            lax.fori_loop(0, batch_rows // tile, one_tile, 0, unroll=True)
            high, low = parts(moved[at_slot], 2)
            total = dot(turned, high) + dot(turned, low)
            after = pl.ds(pl.multiple_of(start + LANES, LANES), LANES)
            sums[h, :, :, after] = sums[h, :, :, after] + total.reshape(ring, cells, LANES)

        fetch(0, 0)

        def two_blocks(i, _):
            b = 2 * i
            fetch(b + 1, 1)
            one_block(b, 0)
            fetch((b + 2) % half_blocks, 0)
            one_block(b + 1, 1)
            return 0

        if not last:
            lax.fori_loop(0, half_blocks // 2, two_blocks, 0)
            return 0
        per_piece = half_blocks // counts[h]
        for p in range(counts[h]):
            lax.fori_loop(p * per_piece // 2, (p + 1) * per_piece // 2, two_blocks, 0)
            send_sums(h, p)

    lax.fori_loop(0, 4, lambda i, _: one_batch(i % 2, i // 2, False), 0)
    lax.fori_loop(2, group, lambda k, _: one_batch(0, k, False), 0)
    for p in range(counts[0]):
        send_sums(0, p)
    lax.fori_loop(2, group - 1, lambda k, _: one_batch(1, k, False), 0)
    one_batch(1, group - 1, True)

    bx, by = c.bx, c.by
    wide = by + 2

    def strips(dx, dy):
        rows_x = range(bx) if dx == 0 else [bx - 1 if dx == 1 else 0]
        row_y, run = (0, by) if dy == 0 else (by - 1 if dy == 1 else 0, 1)
        return [
            ((row + 1) * wide + row_y + 1, (row + 1 - dx * bx) * wide + row_y + 1 - dy * by, run) for row in rows_x
        ]

    strip_list = [(dx, dy) + strip for dx, dy in around for strip in strips(dx, dy)]

    def piece_span(h, p):
        per_piece = half // counts[h]
        return h * half + p * per_piece, per_piece

    def halo_copy(j, n, way=1):
        dx, dy, source, target, run = strip_list[j]
        lanes = pl.ds(*piece_span(*piece_list[n]))
        return pltpu.make_async_remote_copy(
            src_ref=padded.at[pl.ds(source, run), :, lanes], dst_ref=padded.at[pl.ds(target, run), :, lanes],
            send_sem=h_send.at[j * pieces + n], recv_sem=h_recv.at[j * pieces + n],
            device_id=near_id(way * dx, way * dy), device_id_type=MESH,
        )

    folds = [None, None]
    for n, (h, p) in enumerate(piece_list):
        total = sums[h, pl.ds(place_of(h, 0), 1), :, piece_lanes(h, p)][0]
        for k in range(1, ring):
            sum_copy(h, p, k).wait_recv()
            total = total + sums_in[h, k - 1, :, piece_lanes(h, p)]
        if p == 0:
            folds[h] = jnp.maximum(total[:, :1], 1.0)
            total = total[:, LANES:]
        total = total / folds[h]
        first, size = piece_span(h, p)
        for b in range(cells):
            padded[(b // by + 1) * wide + b % by + 1, :, first : first + size] = total[b : b + 1]
        for dx, dy in around:

            @pl.when(valid(dx, dy))
            def _():
                for j, strip in enumerate(strip_list):
                    if strip[:2] == (dx, dy):
                        halo_copy(j, n).start()

    padded_rows = (bx + 2) * wide
    lag_rows = up_to(padded_rows, 8)
    lags = 2 * DIP + 1
    lane = iota((cells, lagged.shape[0]), 1)
    place = iota((cells, 1), 0)
    weights = jnp.zeros(lane.shape, f32)
    for n in range(9):
        for b in range(cells):
            p = (b // by + n // 3) * wide + b % by + n % 3
            spot = p + (dip_ref[b // by, b % by, n] + DIP) * lag_rows
            factor = CENTER_WEIGHT if n == 4 else SIDE_WEIGHT
            weights = weights + jnp.where((place == b) & (lane == spot), factor, 0.0)
    weights = weights.astype(bf16)
    if lagged.shape[0] > lags * lag_rows:
        lagged[lags * lag_rows :, :] = jnp.zeros((lagged.shape[0] - lags * lag_rows, samples), f32)

    for dx, dy in around:
        ok = valid(-dx, -dy)
        mine_in = [j for j, strip in enumerate(strip_list) if strip[:2] == (dx, dy)]

        @pl.when(ok)
        def _():
            for j in mine_in:
                for p in range(pieces):
                    halo_copy(j, p, -1).wait_recv()

        @pl.when(jnp.logical_not(ok))
        def _():
            for j in mine_in:
                target, run = strip_list[j][3:]
                padded[pl.ds(target, run)] = jnp.zeros((run, 1, samples), f32)

    lines = [padded[line] for line in range(padded_rows)]
    lines += [jnp.zeros((1, samples), f32)] * (lag_rows - padded_rows)
    whole = jnp.concatenate(lines, axis=0)
    time = iota((lag_rows, samples), 1)
    for i in range(lags):
        lag = i - DIP
        shifted = whole if lag == 0 else pltpu.roll(whole, (-lag) % samples, 1)
        inside = (time + lag >= 0) & (time + lag < samples)
        lagged[i * lag_rows : (i + 1) * lag_rows, :] = jnp.where(inside, shifted, 0.0)
    result = sum(dot(weights, piece) for piece in parts(lagged[...], 3))
    for row in range(bx):
        out_ref[row] = result[row * by : (row + 1) * by, :]

    def done_plane(k, _):
        for h in range(2):
            meta_copy(h, k).wait_send()
            row_copy(h, k).wait_send()
        return 0

    def done_column(k, _):
        for h in range(2):
            slow_copy(h, k).wait_send()
        for h, p in piece_list:
            sum_copy(h, p, k).wait_send()
        return 0

    lax.fori_loop(1, group, done_plane, 0)
    lax.fori_loop(1, ring, done_column, 0)
    for dx, dy in around:

        @pl.when(valid(dx, dy))
        def _():
            for j, strip in enumerate(strip_list):
                if strip[:2] == (dx, dy):
                    for p in range(pieces):
                        halo_copy(j, p).wait_send()


class Sizes:
    pass


def body(sizes, traces, trace_offset, trace_owner, trace_cell, slowness, band_start, dip_shift):
    c = Sizes()
    size_x, c.nil = sizes
    c.nz = 1
    while c.nz * c.nz < size_x:
        c.nz *= 2
    c.nx = size_x // c.nz
    assert c.nx * 2 == c.nil
    c.group = c.nil
    c.ring = c.nz * c.nx
    count, c.samples = traces.shape
    c.cap = max(2, 5 * count // (4 * size_x * c.nil))
    c.rows = up_to(c.ring * c.cap, 16)
    c.meta_rows = up_to(c.rows, LANES)
    c.bx, c.by = slowness.shape[:2]
    c.counts = (1, 3)
    cells = c.bx * c.by
    bins = c.ring * cells
    samples = c.samples
    blocks = samples // LANES
    batch_rows = c.rows
    half = samples // 2
    cols = half + LANES
    pieces = sum(c.counts)
    lag_rows = up_to((c.bx + 2) * (c.by + 2), 8)
    dma = pltpu.SemaphoreType.DMA
    strip_count = 2 + 2 * c.bx + 4
    return pl.pallas_call(
        functools.partial(kernel, c),
        out_shape=jax.ShapeDtypeStruct((c.bx, c.by, samples), f32),
        in_specs=[pl.BlockSpec(memory_space=pltpu.VMEM)] * 3
        + [pl.BlockSpec(memory_space=pl.ANY)]
        + [pl.BlockSpec(memory_space=pltpu.VMEM)] * 2
        + [pl.BlockSpec(memory_space=pltpu.SMEM)],
        out_specs=pl.BlockSpec(memory_space=pltpu.VMEM),
        scratch_shapes=[
            pltpu.VMEM((count, samples), bf16),
            pltpu.VMEM((cells, samples), f32),
            pltpu.VMEM((1, samples), jnp.int32),
            pltpu.VMEM((2 * c.group, c.rows, cols), bf16),
            pltpu.VMEM((2 * c.group, 16, c.meta_rows), bf16),
            pltpu.VMEM((2 * c.group * c.rows, cols), bf16),
            pltpu.VMEM((2 * c.group, 16, c.meta_rows), bf16),
            pltpu.VMEM((2, c.ring, cells, half), f32),
            pltpu.VMEM((2, 4 * bins, half), bf16),
            pltpu.VMEM((blocks, 2 * LANES, BAND * LANES), bf16),
            pltpu.VMEM((2, batch_rows, BAND * LANES), f32),
            pltpu.VMEM((2, batch_rows, LANES), f32),
            pltpu.VMEM((3, batch_rows, LANES), f32),
            pltpu.VMEM((2, c.ring, cells, cols), f32),
            pltpu.VMEM((2, c.ring - 1, cells, cols), f32),
            pltpu.VMEM(((c.bx + 2) * (c.by + 2), 1, samples), f32),
            pltpu.VMEM((up_to((2 * DIP + 1) * lag_rows, LANES), samples), f32),
            dma, dma((2 * c.group,)), dma((2 * c.group,)), dma((2 * c.group,)), dma((2 * c.group,)),
            dma((2 * c.ring,)), dma((2 * c.ring,)), dma((pieces * c.ring,)), dma((pieces * c.ring,)),
            dma((strip_count * pieces,)), dma((strip_count * pieces,)),
        ],
        compiler_params=pltpu.CompilerParams(
            collective_id=0, has_side_effects=True, vmem_limit_bytes=56 * 1024 * 1024
        ),
        name="bin_stack_smooth",
    )(trace_owner, trace_offset, trace_cell, traces, slowness, band_start, dip_shift.transpose(1, 2, 0))


def solution(mesh):
    sizes = (mesh.shape["xline"], mesh.shape["iline"])
    return jax.shard_map(
        functools.partial(body, sizes),
        mesh=mesh,
        in_specs=(
            P(("xline", "iline"), None),
            P(("xline", "iline")),
            P(("xline", "iline")),
            P(("xline", "iline")),
            P("xline", "iline", None),
            P(),
            P(None, "xline", "iline"),
        ),
        out_specs=P("xline", "iline", None),
        check_vma=False,
    )
```

```python
import functools

import jax
import jax.numpy as jnp
from jax import lax
from jax.experimental import pallas as pl
from jax.experimental.pallas import tpu as pltpu
from jax.sharding import PartitionSpec as P

BAND = 8
DIP = 4
HALF = BAND // 2
LANES = 128
CENTER_WEIGHT = 0.5
SIDE_WEIGHT = 0.0625
MESH = pl.DeviceIdType.MESH
NT_DIMS = (((1,), (1,)), ((), ()))
f32 = jnp.float32
bf16 = jnp.bfloat16


def up_to(value, multiple):
    return -(-value // multiple) * multiple


def iota(shape, dim):
    return lax.broadcasted_iota(jnp.int32, shape, dim)


def dot(a, b):
    return jnp.dot(a, b, preferred_element_type=f32)


def parts(value, count):
    out = []
    for _ in range(count):
        piece = value.astype(bf16)
        out.append(piece)
        value = value - piece.astype(f32)
    return out


def kernel(
    c, owner_ref, offset_ref, cell_ref, traces_hbm, slow_in, band_in, dip_ref, out_ref,
    traces_ref, slow_ref, band_ref, packed, send, send_meta, recv, recv_meta, slows, slow_parts, gather, picks, slow_rows, moved,
    sums, sums_in, padded, lagged,
    t_sem, s_send, s_recv, m_send, m_recv, w_send, w_recv, z_send, z_recv, h_send, h_recv,
):
    nx, nil, nz, group, cap, rows, samples = c.nx, c.nil, c.nz, c.group, c.cap, c.rows, c.samples
    ny = nil // 2
    blocks = samples // LANES
    cells = slow_ref.shape[0]
    xl = lax.axis_index("xline")
    il = lax.axis_index("iline")
    z, x = xl // nx, xl % nx
    y, core = il // 2, il % 2

    def plane(k):
        kx, ky, kc = k // nil, (k % nil) // 2, k % 2
        tx = (x + kx) % nx
        ti = ((y + ky) % ny) * 2 + (core + kc) % 2
        return tx, ti

    def plane_id(k):
        tx, ti = plane(k)
        return {"xline": z * nx + tx, "iline": ti}

    def z_id(k):
        return {"xline": ((z + k) % nz) * nx + x, "iline": il}

    around = [(dx, dy) for dx in (-1, 0, 1) for dy in (-1, 0, 1) if (dx, dy) != (0, 0)]

    def valid(dx, dy):
        ok = None
        for at, step, size in ((xl, dx, nx * nz), (il, dy, nil)):
            if step:
                here = (at + step >= 0) & (at + step < size)
                ok = here if ok is None else ok & here
        return ok

    def near_id(dx, dy):
        return {"xline": xl + dx, "iline": il + dy}

    traces_copy = pltpu.make_async_copy(traces_hbm, traces_ref, t_sem)
    traces_copy.start()

    barrier = pltpu.get_barrier_semaphore()

    def greet(target):
        pl.semaphore_signal(barrier, inc=1, device_id=target, device_id_type=MESH)

    lax.fori_loop(1, group, lambda k, _: (greet(plane_id(k)), 0)[1], 0)
    lax.fori_loop(1, nz, lambda k, _: (greet(z_id(k)), 0)[1], 0)
    for dx, dy in around:
        pl.when(valid(dx, dy))(functools.partial(lambda t: greet(t), near_id(dx, dy)))

    count = traces_ref.shape[0]
    for line in range(c.bx):
        slow_ref[line * c.by : (line + 1) * c.by, :] = slow_in[line]
    band_ref[...] = band_in[...].reshape(1, samples)
    owner_row = owner_ref[...].reshape(1, count).astype(f32)
    turn = jnp.floor((owner_row + 0.5) * (1.0 / group))
    chunk_row = owner_row - turn * group
    inner_row = turn * cap
    offset_row = offset_ref[...].astype(f32).reshape(1, count)
    cell_row = cell_ref[...].reshape(1, count).astype(f32) + 1.0
    owners = up_to(group * nz, 16)
    mine = jnp.where(iota((owners, count), 0).astype(f32) == owner_row, 1.0, 0.0)
    earlier = jnp.where(iota((count, count), 0) < iota((count, count), 1), 1.0, 0.0).astype(bf16)
    before = dot(mine.astype(bf16), earlier)
    inner_row = inner_row + jnp.sum(mine * before, axis=0, keepdims=True)
    values = jnp.concatenate([offset_row, cell_row, jnp.zeros((14, count), f32)], axis=0).astype(bf16)

    def span_of(at, size):
        return 3 - jnp.where(at == 0, 1, 0) - jnp.where(at == size - 1, 1, 0)

    near = span_of(xl, nx * nz) * span_of(il, nil) - 1
    pl.semaphore_wait(barrier, (group - 1) + (nz - 1) + near)

    def slow_copy(k):
        return pltpu.make_async_remote_copy(
            src_ref=slow_ref, dst_ref=slows.at[z], send_sem=w_send.at[k], recv_sem=w_recv.at[k],
            device_id=z_id(k), device_id_type=MESH,
        )

    def chunk_of(k):
        tx, ti = plane(k)
        return tx * nil + ti

    def row_copy(k):
        return pltpu.make_async_remote_copy(
            src_ref=send.at[chunk_of(k)], dst_ref=recv.at[pl.ds(pl.multiple_of(k * rows, 16), rows), pl.ds(0, samples)],
            send_sem=s_send.at[k], recv_sem=s_recv.at[k], device_id=plane_id(k), device_id_type=MESH,
        )

    def meta_copy(k):
        return pltpu.make_async_remote_copy(
            src_ref=send_meta.at[chunk_of(k)], dst_ref=recv_meta.at[k],
            send_sem=m_send.at[k], recv_sem=m_recv.at[k], device_id=plane_id(k), device_id_type=MESH,
        )

    lax.fori_loop(1, nz, lambda k, _: (slow_copy(k).start(), 0)[1], 0)

    def one_hot(step):
        place = iota((group * step, count), 0).astype(f32)
        return jnp.where(place == chunk_row * step + inner_row, 1.0, 0.0).astype(bf16)

    info = lax.dot_general(values, one_hot(c.meta_rows), NT_DIMS, preferred_element_type=f32).astype(bf16)
    for k in range(group):
        send_meta[k] = info[:, k * c.meta_rows : (k + 1) * c.meta_rows]
    traces_copy.wait()
    packed[...] = dot(one_hot(rows), traces_ref[...])

    def turn_chunk(k, _):
        chunk = packed[pl.ds(pl.multiple_of(k * rows, 16), rows), :]
        send[k] = pltpu.roll(chunk, LANES // 2, 1).astype(bf16)
        return 0

    lax.fori_loop(0, group, turn_chunk, 0)

    def send_one(k, _):
        meta_copy(k).start()
        row_copy(k).start()
        return 0

    lax.fori_loop(1, group, send_one, 0)
    recv[0:rows, 0:samples] = send[pl.ds(chunk_of(0), 1)][0]
    recv_meta[0] = send_meta[pl.ds(chunk_of(0), 1)][0]

    low = (LANES // 2 - BAND) // 16 * 16
    high = up_to(LANES + LANES // 2 + BAND, 16)

    def make_gather(b, _):
        gather[b, :low, :] = jnp.zeros((low, BAND * LANES), bf16)
        gather[b, high:, :] = jnp.zeros((2 * LANES - high, BAND * LANES), bf16)
        start = pl.multiple_of(b * LANES, LANES)
        position = band_ref[:, pl.ds(start, LANES)] - start + LANES // 2
        window = iota((high - low, LANES), 0) + low
        for pair in range(HALF):
            first = jnp.where(window == position + pair, 1.0, 0.0)
            last = jnp.where(window == position + (BAND - 1 - pair), 1.0, 0.0)
            at = pair * 2 * LANES
            gather[b, low:high, at : at + LANES] = (first + last).astype(bf16)
            gather[b, low:high, at + LANES : at + 2 * LANES] = ((first - last) * float(BAND - 1 - 2 * pair)).astype(bf16)
        return 0

    lax.fori_loop(0, blocks, make_gather, 0)

    slows[pl.ds(z, 1)] = slow_ref[...][None]
    lax.fori_loop(1, nz, lambda k, _: (slow_copy(k).wait_recv(), 0)[1], 0)
    bins = nz * cells
    table = slows[...].reshape(bins, samples)
    for i, piece in enumerate(parts(table, 3)):
        slow_parts[i * bins : (i + 1) * bins, :] = piece
    slow_parts[3 * bins :, :] = jnp.zeros((bins, samples), bf16)

    sums[...] = jnp.zeros_like(sums)
    pieces = c.pieces
    per_piece = blocks // pieces

    def piece_lanes(p):
        first = 0 if p == 0 else LANES + p * per_piece * LANES
        return pl.ds(first, LANES + (p + 1) * per_piece * LANES - first)

    def sum_copy(k, p):
        return pltpu.make_async_remote_copy(
            src_ref=sums.at[(z + k) % nz, :, piece_lanes(p)], dst_ref=sums_in.at[k - 1, :, piece_lanes(p)],
            send_sem=z_send.at[k * pieces + p], recv_sem=z_recv.at[k * pieces + p],
            device_id=z_id(k), device_id_type=MESH,
        )

    def one_batch(first, batch, last):
        batch_rows = batch * rows
        tile = 32 if batch_rows % 32 == 0 else 16
        for j in range(batch):
            k = first + j
            if k > 0:
                meta_copy(k).wait_recv()
                row_copy(k).wait_recv()

        span = pl.ds(first * rows, batch_rows)
        recv[span, samples : samples + LANES] = recv[span, 0:LANES]
        same = jnp.where(iota((rows, c.meta_rows), 0) == iota((rows, c.meta_rows), 1), 1.0, 0.0).astype(bf16)
        columns = jnp.concatenate(
            [
                lax.dot_general(same, recv_meta[first + j], NT_DIMS, preferred_element_type=f32)
                for j in range(batch)
            ],
            axis=0,
        )
        offset = columns[:, 0:1]
        cell = columns[:, 1:2]
        step = iota((batch_rows, 1), 0)
        base = jnp.zeros((batch_rows, 1), f32)
        for j in range(batch):
            for owner in range(1, nz):
                base = base + jnp.where((step >= j * rows + owner * cap) & (step < (j + 1) * rows), float(cells), 0.0)
        bin_id = jnp.where(cell > 0.5, base + cell - 1.0, -1.0)
        lane = iota((1, 4 * bins), 1)
        members = jnp.where((lane % bins).astype(f32) == bin_id, 1.0, 0.0).astype(bf16)
        eye = jnp.where(iota((bins, 4 * bins), 0) == iota((bins, 4 * bins), 1), 1.0, 0.0).astype(bf16)
        turned = lax.dot_general(eye, members, NT_DIMS, preferred_element_type=f32)
        fold = jnp.sum(turned, axis=1, keepdims=True)
        turned = turned.astype(bf16)
        head = pl.ds(0, LANES)
        sums[:, :, head] = sums[:, :, head] + jnp.broadcast_to(fold, (bins, LANES)).reshape(nz, cells, LANES)
        offset2 = jnp.broadcast_to(offset * offset, (batch_rows, LANES))
        moved[2, :batch_rows] = offset2

        def fetch(b, at):
            start = pl.multiple_of(b * LANES, LANES)
            picks[at, :batch_rows] = dot(recv[span, pl.ds(start, 2 * LANES)], gather[b])
            slow_rows[at, :batch_rows] = dot(members, slow_parts[:, pl.ds(start, LANES)])

        def one_block(b, at_slot):
            start = pl.multiple_of(b * LANES, LANES)
            lanes = pl.ds(start, LANES)
            time = (iota((1, LANES), 1) + start).astype(f32)
            time2 = time * time
            center = band_ref[:, lanes].astype(f32) + 0.5 * (BAND - 1) - time

            def one_tile(r, _):
                here = pl.ds(pl.multiple_of(r * tile, 16), tile)
                delay2 = moved[2, here, :] * slow_rows[at_slot, here, :]
                square = jnp.maximum(time2 + delay2, 1e-30)
                off = center - delay2 * pl.reciprocal(time + square * lax.rsqrt(square), approx=True)
                u = off * off
                u2 = u * u
                terms = []
                for pair in range(HALF):
                    reach = 0.5 * (BAND - 1) - pair
                    at = pair * 2 * LANES
                    v = u + (1.0 + reach * reach)
                    n = v * picks[at_slot, here, at : at + LANES] + off * picks[at_slot, here, at + LANES : at + 2 * LANES]
                    q = u2 + ((2.0 - 2.0 * reach * reach) * u + (1.0 + reach * reach) ** 2)
                    terms.append((n, v, q))
                while len(terms) > 1:
                    merged = []
                    for (n1, v1, q1), (n2, v2, q2) in zip(terms[::2], terms[1::2]):
                        q = None if len(terms) == 2 else q1 * q2
                        merged.append((n1 * q2 + n2 * q1, v1 * q2 + v2 * q1, q))
                    terms = merged
                n, v, _q = terms[0]
                v = v + v
                inverse = pl.reciprocal(v, approx=True)
                moved[at_slot, here, :] = n * (inverse * (2.0 - v * inverse))
                return 0

            lax.fori_loop(0, batch_rows // tile, one_tile, 0, unroll=True)
            high, low = parts(moved[at_slot, :batch_rows], 2)
            total = dot(turned, high) + dot(turned, low)
            after = pl.ds(pl.multiple_of(start + LANES, LANES), LANES)
            sums[:, :, after] = sums[:, :, after] + total.reshape(nz, cells, LANES)

        fetch(0, 0)

        def two_blocks(i, _):
            b = 2 * i
            fetch(b + 1, 1)
            one_block(b, 0)
            fetch((b + 2) % blocks, 0)
            one_block(b + 1, 1)
            return 0

        if not last:
            lax.fori_loop(0, blocks // 2, two_blocks, 0)
            return 0
        for p in range(pieces):
            lax.fori_loop(p * per_piece // 2, (p + 1) * per_piece // 2, two_blocks, 0)
            for k in range(1, nz):
                sum_copy(k, p).start()

    first = 0
    for batch in c.batches:
        one_batch(first, batch, first + batch == group)
        first += batch

    bx, by = c.bx, c.by
    wide = by + 2

    def strips(dx, dy):
        rows_x = range(bx) if dx == 0 else [bx - 1 if dx == 1 else 0]
        row_y, run = (0, by) if dy == 0 else (by - 1 if dy == 1 else 0, 1)
        return [
            ((row + 1) * wide + row_y + 1, (row + 1 - dx * bx) * wide + row_y + 1 - dy * by, run) for row in rows_x
        ]

    strip_list = [(dx, dy) + strip for dx, dy in around for strip in strips(dx, dy)]

    def halo_copy(j, p, way=1):
        dx, dy, source, target, run = strip_list[j]
        lanes = pl.ds(p * per_piece * LANES, per_piece * LANES)
        return pltpu.make_async_remote_copy(
            src_ref=padded.at[pl.ds(source, run), :, lanes], dst_ref=padded.at[pl.ds(target, run), :, lanes],
            send_sem=h_send.at[j * pieces + p], recv_sem=h_recv.at[j * pieces + p],
            device_id=near_id(way * dx, way * dy), device_id_type=MESH,
        )

    fold = None
    for p in range(pieces):
        total = sums[pl.ds(z, 1), :, piece_lanes(p)][0]
        for k in range(1, nz):
            sum_copy(k, p).wait_recv()
            total = total + sums_in[k - 1, :, piece_lanes(p)]
        if p == 0:
            fold = jnp.maximum(total[:, :1], 1.0)
            total = total[:, LANES:]
        total = total / fold
        for b in range(cells):
            padded[(b // by + 1) * wide + b % by + 1, :, p * per_piece * LANES : (p + 1) * per_piece * LANES] = total[b : b + 1]
        for dx, dy in around:

            @pl.when(valid(dx, dy))
            def _():
                for j, strip in enumerate(strip_list):
                    if strip[:2] == (dx, dy):
                        halo_copy(j, p).start()

    padded_rows = (bx + 2) * wide
    lag_rows = up_to(padded_rows, 8)
    lags = 2 * DIP + 1
    lane = iota((cells, lagged.shape[0]), 1)
    place = iota((cells, 1), 0)
    weights = jnp.zeros(lane.shape, f32)
    for n in range(9):
        for b in range(cells):
            p = (b // by + n // 3) * wide + b % by + n % 3
            spot = p + (dip_ref[b // by, b % by, n] + DIP) * lag_rows
            factor = CENTER_WEIGHT if n == 4 else SIDE_WEIGHT
            weights = weights + jnp.where((place == b) & (lane == spot), factor, 0.0)
    weights = weights.astype(bf16)
    if lagged.shape[0] > lags * lag_rows:
        lagged[lags * lag_rows :, :] = jnp.zeros((lagged.shape[0] - lags * lag_rows, samples), f32)

    for dx, dy in around:
        ok = valid(-dx, -dy)
        mine_in = [j for j, strip in enumerate(strip_list) if strip[:2] == (dx, dy)]

        @pl.when(ok)
        def _():
            for j in mine_in:
                for p in range(pieces):
                    halo_copy(j, p, -1).wait_recv()

        @pl.when(jnp.logical_not(ok))
        def _():
            for j in mine_in:
                target, run = strip_list[j][3:]
                padded[pl.ds(target, run)] = jnp.zeros((run, 1, samples), f32)

    lines = [padded[line] for line in range(padded_rows)]
    lines += [jnp.zeros((1, samples), f32)] * (lag_rows - padded_rows)
    whole = jnp.concatenate(lines, axis=0)
    time = iota((lag_rows, samples), 1)
    for i in range(lags):
        lag = i - DIP
        shifted = whole if lag == 0 else pltpu.roll(whole, (-lag) % samples, 1)
        inside = (time + lag >= 0) & (time + lag < samples)
        lagged[i * lag_rows : (i + 1) * lag_rows, :] = jnp.where(inside, shifted, 0.0)
    result = sum(dot(weights, piece) for piece in parts(lagged[...], 3))
    for row in range(bx):
        out_ref[row] = result[row * by : (row + 1) * by, :]

    def done_plane(k, _):
        meta_copy(k).wait_send()
        row_copy(k).wait_send()
        return 0

    def done_z(k, _):
        slow_copy(k).wait_send()
        for p in range(pieces):
            sum_copy(k, p).wait_send()
        return 0

    lax.fori_loop(1, group, done_plane, 0)
    lax.fori_loop(1, nz, done_z, 0)
    for dx, dy in around:

        @pl.when(valid(dx, dy))
        def _():
            for j, strip in enumerate(strip_list):
                if strip[:2] == (dx, dy):
                    for p in range(pieces):
                        halo_copy(j, p).wait_send()


class Sizes:
    pass


def body(sizes, traces, trace_offset, trace_owner, trace_cell, slowness, band_start, dip_shift):
    c = Sizes()
    size_x, c.nil = sizes
    c.nz = 1
    while c.nz * c.nz < size_x:
        c.nz *= 2
    c.nx = size_x // c.nz
    c.group = c.nx * c.nil
    count, c.samples = traces.shape
    c.cap = max(2, 5 * count // (4 * size_x * c.nil))
    c.rows = up_to(c.nz * c.cap, 16)
    c.meta_rows = up_to(c.rows, LANES)
    c.bx, c.by = slowness.shape[:2]
    c.batches = (c.group // 4, c.group // 2, c.group // 4)
    c.pieces = 3
    cells = c.bx * c.by
    bins = c.nz * cells
    samples = c.samples
    blocks = samples // LANES
    batch_rows = max(c.batches) * c.rows
    lag_rows = up_to((c.bx + 2) * (c.by + 2), 8)
    dma = pltpu.SemaphoreType.DMA
    strip_count = 2 + 2 * c.bx + 4
    return pl.pallas_call(
        functools.partial(kernel, c),
        out_shape=jax.ShapeDtypeStruct((c.bx, c.by, samples), f32),
        in_specs=[pl.BlockSpec(memory_space=pltpu.VMEM)] * 3
        + [pl.BlockSpec(memory_space=pl.ANY)]
        + [pl.BlockSpec(memory_space=pltpu.VMEM)] * 2
        + [pl.BlockSpec(memory_space=pltpu.SMEM)],
        out_specs=pl.BlockSpec(memory_space=pltpu.VMEM),
        scratch_shapes=[
            pltpu.VMEM((count, samples), bf16),
            pltpu.VMEM((cells, samples), f32),
            pltpu.VMEM((1, samples), jnp.int32),
            pltpu.VMEM((c.group * c.rows, samples), f32),
            pltpu.VMEM((c.group, c.rows, samples), bf16),
            pltpu.VMEM((c.group, 16, c.meta_rows), bf16),
            pltpu.VMEM((c.group * c.rows, samples + LANES), bf16),
            pltpu.VMEM((c.group, 16, c.meta_rows), bf16),
            pltpu.VMEM((c.nz, cells, samples), f32),
            pltpu.VMEM((4 * bins, samples), bf16),
            pltpu.VMEM((blocks, 2 * LANES, BAND * LANES), bf16),
            pltpu.VMEM((2, batch_rows, BAND * LANES), f32),
            pltpu.VMEM((2, batch_rows, LANES), f32),
            pltpu.VMEM((3, batch_rows, LANES), f32),
            pltpu.VMEM((c.nz, cells, samples + LANES), f32),
            pltpu.VMEM((c.nz - 1, cells, samples + LANES), f32),
            pltpu.VMEM(((c.bx + 2) * (c.by + 2), 1, samples), f32),
            pltpu.VMEM((up_to((2 * DIP + 1) * lag_rows, LANES), samples), f32),
            dma, dma((c.group,)), dma((c.group,)), dma((c.group,)), dma((c.group,)),
            dma((c.nz,)), dma((c.nz,)), dma((c.nz * c.pieces,)), dma((c.nz * c.pieces,)),
            dma((strip_count * c.pieces,)), dma((strip_count * c.pieces,)),
        ],
        compiler_params=pltpu.CompilerParams(
            collective_id=0, has_side_effects=True, vmem_limit_bytes=56 * 1024 * 1024
        ),
        name="bin_stack_smooth",
    )(trace_owner, trace_offset, trace_cell, traces, slowness, band_start, dip_shift.transpose(1, 2, 0))


def solution(mesh):
    sizes = (mesh.shape["xline"], mesh.shape["iline"])
    return jax.shard_map(
        functools.partial(body, sizes),
        mesh=mesh,
        in_specs=(
            P(("xline", "iline"), None),
            P(("xline", "iline")),
            P(("xline", "iline")),
            P(("xline", "iline")),
            P("xline", "iline", None),
            P(),
            P(None, "xline", "iline"),
        ),
        out_specs=P("xline", "iline", None),
        check_vma=False,
    )
```

```python
import functools

import jax
import jax.numpy as jnp
from jax import lax
from jax.experimental import pallas as pl
from jax.experimental.pallas import tpu as pltpu
from jax.sharding import PartitionSpec as P

BAND = 8
DIP = 4
HALF = BAND // 2
LANES = 128
CENTER_WEIGHT = 0.5
SIDE_WEIGHT = 0.0625
MESH = pl.DeviceIdType.MESH
NT_DIMS = (((1,), (1,)), ((), ()))
f32 = jnp.float32
bf16 = jnp.bfloat16


def up_to(value, multiple):
    return -(-value // multiple) * multiple


def iota(shape, dim):
    return lax.broadcasted_iota(jnp.int32, shape, dim)


def dot(a, b):
    return jnp.dot(a, b, preferred_element_type=f32)


def parts(value, count):
    out = []
    for _ in range(count):
        piece = value.astype(bf16)
        out.append(piece)
        value = value - piece.astype(f32)
    return out


def kernel(
    c, owner_ref, offset_ref, cell_ref, traces_hbm, slow_in, band_in, dip_ref, out_ref,
    traces_ref, slow_ref, band_ref, send, send_meta, recv, recv_meta, slows, slow_parts, gather, picks, slow_rows, moved,
    sums, sums_in, padded, lagged,
    t_sem, s_send, s_recv, m_send, m_recv, w_send, w_recv, z_send, z_recv, h_send, h_recv,
):
    nx, nil, nz, group, cap, rows, samples = c.nx, c.nil, c.nz, c.group, c.cap, c.rows, c.samples
    ny = nil // 2
    blocks = samples // LANES
    cells = slow_ref.shape[0]
    xl = lax.axis_index("xline")
    il = lax.axis_index("iline")
    z, x = xl // nx, xl % nx
    y, core = il // 2, il % 2

    def plane(k):
        kx, ky, kc = k // nil, (k % nil) // 2, k % 2
        tx = (x + kx) % nx
        ti = ((y + ky) % ny) * 2 + (core + kc) % 2
        return tx, ti

    def plane_id(k):
        tx, ti = plane(k)
        return {"xline": z * nx + tx, "iline": ti}

    def z_id(k):
        return {"xline": ((z + k) % nz) * nx + x, "iline": il}

    around = [(dx, dy) for dx in (-1, 0, 1) for dy in (-1, 0, 1) if (dx, dy) != (0, 0)]

    def valid(dx, dy):
        ok = None
        for at, step, size in ((xl, dx, nx * nz), (il, dy, nil)):
            if step:
                here = (at + step >= 0) & (at + step < size)
                ok = here if ok is None else ok & here
        return ok

    def near_id(dx, dy):
        return {"xline": xl + dx, "iline": il + dy}

    traces_copy = pltpu.make_async_copy(traces_hbm, traces_ref, t_sem)
    traces_copy.start()

    barrier = pltpu.get_barrier_semaphore()

    def greet(target):
        pl.semaphore_signal(barrier, inc=1, device_id=target, device_id_type=MESH)

    lax.fori_loop(1, group, lambda k, _: (greet(plane_id(k)), 0)[1], 0)
    lax.fori_loop(1, nz, lambda k, _: (greet(z_id(k)), 0)[1], 0)
    for dx, dy in around:
        pl.when(valid(dx, dy))(functools.partial(lambda t: greet(t), near_id(dx, dy)))

    count = traces_ref.shape[0]
    for line in range(c.bx):
        slow_ref[line * c.by : (line + 1) * c.by, :] = slow_in[line]
    band_ref[...] = band_in[...].reshape(1, samples)
    owner_row = owner_ref[...].reshape(1, count).astype(f32)
    turn = jnp.floor((owner_row + 0.5) * (1.0 / group))
    base_row = (owner_row - turn * group) * rows + turn * cap
    offset_row = offset_ref[...].astype(f32).reshape(1, count)
    cell_row = cell_ref[...].reshape(1, count).astype(f32) + 1.0
    owners = up_to(group * nz, 16)
    mine = jnp.where(iota((owners, count), 0).astype(f32) == owner_row, 1.0, 0.0)
    earlier = jnp.where(iota((count, count), 0) < iota((count, count), 1), 1.0, 0.0).astype(bf16)
    before = dot(mine.astype(bf16), earlier)
    slot = base_row + jnp.sum(mine * before, axis=0, keepdims=True)
    values = jnp.concatenate([offset_row, cell_row, jnp.zeros((14, count), f32)], axis=0).astype(bf16)

    def span_of(at, size):
        return 3 - jnp.where(at == 0, 1, 0) - jnp.where(at == size - 1, 1, 0)

    near = span_of(xl, nx * nz) * span_of(il, nil) - 1
    pl.semaphore_wait(barrier, (group - 1) + (nz - 1) + near)

    def slow_copy(k):
        return pltpu.make_async_remote_copy(
            src_ref=slow_ref, dst_ref=slows.at[z], send_sem=w_send.at[k], recv_sem=w_recv.at[k],
            device_id=z_id(k), device_id_type=MESH,
        )

    def row_copy(k):
        return pltpu.make_async_remote_copy(
            src_ref=send.at[k], dst_ref=recv.at[pl.ds(pl.multiple_of(k * rows, 16), rows), pl.ds(0, samples)],
            send_sem=s_send.at[k], recv_sem=s_recv.at[k], device_id=plane_id(k), device_id_type=MESH,
        )

    def meta_copy(k):
        return pltpu.make_async_remote_copy(
            src_ref=send_meta.at[k], dst_ref=recv_meta.at[k],
            send_sem=m_send.at[k], recv_sem=m_recv.at[k], device_id=plane_id(k), device_id_type=MESH,
        )

    lax.fori_loop(1, nz, lambda k, _: (slow_copy(k).start(), 0)[1], 0)

    def pack(k):
        tx, ti = plane(k)
        first = ((tx * nil + ti) * rows).astype(f32)
        hot = jnp.where(iota((c.meta_rows, count), 0).astype(f32) + first == slot, 1.0, 0.0).astype(bf16)
        chunk = dot(hot[:rows], traces_ref[...])
        chunk = pltpu.roll(chunk, LANES // 2, 1).astype(bf16)
        info = lax.dot_general(values, hot, NT_DIMS, preferred_element_type=f32).astype(bf16)
        return chunk, info

    def send_one(k, _):
        chunk, info = pack(k)
        send[k] = chunk
        send_meta[k] = info
        meta_copy(k).start()
        row_copy(k).start()
        return 0

    traces_copy.wait()
    lax.fori_loop(1, group, send_one, 0)
    chunk, info = pack(0)
    recv[0:rows, 0:samples] = chunk
    recv_meta[0] = info

    low = (LANES // 2 - BAND) // 16 * 16
    high = up_to(LANES + LANES // 2 + BAND, 16)

    def make_gather(b, _):
        gather[b, :low, :] = jnp.zeros((low, BAND * LANES), bf16)
        gather[b, high:, :] = jnp.zeros((2 * LANES - high, BAND * LANES), bf16)
        start = pl.multiple_of(b * LANES, LANES)
        position = band_ref[:, pl.ds(start, LANES)] - start + LANES // 2
        window = iota((high - low, LANES), 0) + low
        for pair in range(HALF):
            first = jnp.where(window == position + pair, 1.0, 0.0)
            last = jnp.where(window == position + (BAND - 1 - pair), 1.0, 0.0)
            at = pair * 2 * LANES
            gather[b, low:high, at : at + LANES] = (first + last).astype(bf16)
            gather[b, low:high, at + LANES : at + 2 * LANES] = ((first - last) * float(BAND - 1 - 2 * pair)).astype(bf16)
        return 0

    lax.fori_loop(0, blocks, make_gather, 0)

    slows[pl.ds(z, 1)] = slow_ref[...][None]
    lax.fori_loop(1, nz, lambda k, _: (slow_copy(k).wait_recv(), 0)[1], 0)
    bins = nz * cells
    table = slows[...].reshape(bins, samples)
    for i, piece in enumerate(parts(table, 3)):
        slow_parts[i * bins : (i + 1) * bins, :] = piece
    slow_parts[3 * bins :, :] = jnp.zeros((bins, samples), bf16)

    sums[...] = jnp.zeros_like(sums)
    batch = c.batch
    batch_rows = batch * rows
    tile = 16

    pieces = c.pieces
    per_piece = blocks // pieces

    def piece_lanes(p):
        first = 0 if p == 0 else LANES + p * per_piece * LANES
        return pl.ds(first, LANES + (p + 1) * per_piece * LANES - first)

    def sum_copy(k, p):
        return pltpu.make_async_remote_copy(
            src_ref=sums.at[(z + k) % nz, :, piece_lanes(p)], dst_ref=sums_in.at[k - 1, :, piece_lanes(p)],
            send_sem=z_send.at[k * pieces + p], recv_sem=z_recv.at[k * pieces + p],
            device_id=z_id(k), device_id_type=MESH,
        )

    def one_batch(i, last):
        for j in range(batch):
            k = i * batch + j

            @pl.when(k > 0)
            def _():
                meta_copy(k).wait_recv()
                row_copy(k).wait_recv()

        span = pl.ds(pl.multiple_of(i * batch_rows, 16), batch_rows)
        recv[span, samples : samples + LANES] = recv[span, 0:LANES]
        same = jnp.where(iota((rows, c.meta_rows), 0) == iota((rows, c.meta_rows), 1), 1.0, 0.0).astype(bf16)
        columns = jnp.concatenate(
            [
                lax.dot_general(same, recv_meta[i * batch + j], NT_DIMS, preferred_element_type=f32)
                for j in range(batch)
            ],
            axis=0,
        )
        offset = columns[:, 0:1]
        cell = columns[:, 1:2]
        step = iota((batch_rows, 1), 0)
        base = jnp.zeros((batch_rows, 1), f32)
        for j in range(batch):
            for owner in range(1, nz):
                base = base + jnp.where((step >= j * rows + owner * cap) & (step < (j + 1) * rows), float(cells), 0.0)
        bin_id = jnp.where(cell > 0.5, base + cell - 1.0, -1.0)
        lane = iota((1, 4 * bins), 1)
        members = jnp.where((lane % bins).astype(f32) == bin_id, 1.0, 0.0).astype(bf16)
        eye = jnp.where(iota((bins, 4 * bins), 0) == iota((bins, 4 * bins), 1), 1.0, 0.0).astype(bf16)
        turned = lax.dot_general(eye, members, NT_DIMS, preferred_element_type=f32)
        fold = jnp.sum(turned, axis=1, keepdims=True)
        turned = turned.astype(bf16)
        head = pl.ds(0, LANES)
        sums[:, :, head] = sums[:, :, head] + jnp.broadcast_to(fold, (bins, LANES)).reshape(nz, cells, LANES)
        offset2 = jnp.broadcast_to(offset * offset, (batch_rows, LANES))
        moved[2] = offset2

        def fetch(b, at):
            start = pl.multiple_of(b * LANES, LANES)
            picks[at] = dot(recv[span, pl.ds(start, 2 * LANES)], gather[b])
            slow_rows[at] = dot(members, slow_parts[:, pl.ds(start, LANES)])

        def one_block(b, at_slot):
            start = pl.multiple_of(b * LANES, LANES)
            lanes = pl.ds(start, LANES)
            time = (iota((1, LANES), 1) + start).astype(f32)
            time2 = time * time
            center = band_ref[:, lanes].astype(f32) + 0.5 * (BAND - 1) - time

            def one_tile(r, _):
                here = pl.ds(pl.multiple_of(r * tile, 16), tile)
                delay2 = moved[2, here, :] * slow_rows[at_slot, here, :]
                square = jnp.maximum(time2 + delay2, 1e-30)
                off = center - delay2 * pl.reciprocal(time + square * lax.rsqrt(square), approx=True)
                u = off * off
                u2 = u * u
                terms = []
                for pair in range(HALF):
                    reach = 0.5 * (BAND - 1) - pair
                    at = pair * 2 * LANES
                    v = u + (1.0 + reach * reach)
                    n = v * picks[at_slot, here, at : at + LANES] + off * picks[at_slot, here, at + LANES : at + 2 * LANES]
                    q = u2 + ((2.0 - 2.0 * reach * reach) * u + (1.0 + reach * reach) ** 2)
                    terms.append((n, v, q))
                while len(terms) > 1:
                    merged = []
                    for (n1, v1, q1), (n2, v2, q2) in zip(terms[::2], terms[1::2]):
                        q = None if len(terms) == 2 else q1 * q2
                        merged.append((n1 * q2 + n2 * q1, v1 * q2 + v2 * q1, q))
                    terms = merged
                n, v, _q = terms[0]
                v = v + v
                inverse = pl.reciprocal(v, approx=True)
                moved[at_slot, here, :] = n * (inverse * (2.0 - v * inverse))
                return 0

            lax.fori_loop(0, batch_rows // tile, one_tile, 0, unroll=True)
            high, low = parts(moved[at_slot], 2)
            total = dot(turned, high) + dot(turned, low)
            after = pl.ds(pl.multiple_of(start + LANES, LANES), LANES)
            sums[:, :, after] = sums[:, :, after] + total.reshape(nz, cells, LANES)

        fetch(0, 0)

        def two_blocks(i, _):
            b = 2 * i
            fetch(b + 1, 1)
            one_block(b, 0)
            fetch((b + 2) % blocks, 0)
            one_block(b + 1, 1)
            return 0

        if not last:
            lax.fori_loop(0, blocks // 2, two_blocks, 0)
            return 0
        for p in range(pieces):
            lax.fori_loop(p * per_piece // 2, (p + 1) * per_piece // 2, two_blocks, 0)
            for k in range(1, nz):
                sum_copy(k, p).start()

    lax.fori_loop(0, group // batch - 1, lambda i, _: one_batch(i, False), 0)
    one_batch(group // batch - 1, True)

    bx, by = c.bx, c.by
    wide = by + 2

    def strips(dx, dy):
        rows_x = range(bx) if dx == 0 else [bx - 1 if dx == 1 else 0]
        row_y, run = (0, by) if dy == 0 else (by - 1 if dy == 1 else 0, 1)
        return [
            ((row + 1) * wide + row_y + 1, (row + 1 - dx * bx) * wide + row_y + 1 - dy * by, run) for row in rows_x
        ]

    strip_list = [(dx, dy) + strip for dx, dy in around for strip in strips(dx, dy)]

    def halo_copy(j, p, way=1):
        dx, dy, source, target, run = strip_list[j]
        lanes = pl.ds(p * per_piece * LANES, per_piece * LANES)
        return pltpu.make_async_remote_copy(
            src_ref=padded.at[pl.ds(source, run), :, lanes], dst_ref=padded.at[pl.ds(target, run), :, lanes],
            send_sem=h_send.at[j * pieces + p], recv_sem=h_recv.at[j * pieces + p],
            device_id=near_id(way * dx, way * dy), device_id_type=MESH,
        )

    fold = None
    for p in range(pieces):
        total = sums[pl.ds(z, 1), :, piece_lanes(p)][0]
        for k in range(1, nz):
            sum_copy(k, p).wait_recv()
            total = total + sums_in[k - 1, :, piece_lanes(p)]
        if p == 0:
            fold = jnp.maximum(total[:, :1], 1.0)
            total = total[:, LANES:]
        total = total / fold
        for b in range(cells):
            padded[(b // by + 1) * wide + b % by + 1, :, p * per_piece * LANES : (p + 1) * per_piece * LANES] = total[b : b + 1]
        for dx, dy in around:

            @pl.when(valid(dx, dy))
            def _():
                for j, strip in enumerate(strip_list):
                    if strip[:2] == (dx, dy):
                        halo_copy(j, p).start()

    padded_rows = (bx + 2) * wide
    lag_rows = up_to(padded_rows, 8)
    lags = 2 * DIP + 1
    lane = iota((cells, lagged.shape[0]), 1)
    place = iota((cells, 1), 0)
    weights = jnp.zeros(lane.shape, f32)
    for n in range(9):
        for b in range(cells):
            p = (b // by + n // 3) * wide + b % by + n % 3
            spot = p + (dip_ref[b // by, b % by, n] + DIP) * lag_rows
            factor = CENTER_WEIGHT if n == 4 else SIDE_WEIGHT
            weights = weights + jnp.where((place == b) & (lane == spot), factor, 0.0)
    weights = weights.astype(bf16)
    if lagged.shape[0] > lags * lag_rows:
        lagged[lags * lag_rows :, :] = jnp.zeros((lagged.shape[0] - lags * lag_rows, samples), f32)

    for dx, dy in around:
        ok = valid(-dx, -dy)
        mine_in = [j for j, strip in enumerate(strip_list) if strip[:2] == (dx, dy)]

        @pl.when(ok)
        def _():
            for j in mine_in:
                for p in range(pieces):
                    halo_copy(j, p, -1).wait_recv()

        @pl.when(jnp.logical_not(ok))
        def _():
            for j in mine_in:
                target, run = strip_list[j][3:]
                padded[pl.ds(target, run)] = jnp.zeros((run, 1, samples), f32)

    lines = [padded[line] for line in range(padded_rows)]
    lines += [jnp.zeros((1, samples), f32)] * (lag_rows - padded_rows)
    whole = jnp.concatenate(lines, axis=0)
    time = iota((lag_rows, samples), 1)
    for i in range(lags):
        lag = i - DIP
        shifted = whole if lag == 0 else pltpu.roll(whole, (-lag) % samples, 1)
        inside = (time + lag >= 0) & (time + lag < samples)
        lagged[i * lag_rows : (i + 1) * lag_rows, :] = jnp.where(inside, shifted, 0.0)
    result = sum(dot(weights, piece) for piece in parts(lagged[...], 2))
    for row in range(bx):
        out_ref[row] = result[row * by : (row + 1) * by, :]

    def done_plane(k, _):
        meta_copy(k).wait_send()
        row_copy(k).wait_send()
        return 0

    def done_z(k, _):
        slow_copy(k).wait_send()
        for p in range(pieces):
            sum_copy(k, p).wait_send()
        return 0

    lax.fori_loop(1, group, done_plane, 0)
    lax.fori_loop(1, nz, done_z, 0)
    for dx, dy in around:

        @pl.when(valid(dx, dy))
        def _():
            for j, strip in enumerate(strip_list):
                if strip[:2] == (dx, dy):
                    for p in range(pieces):
                        halo_copy(j, p).wait_send()


class Sizes:
    pass


def body(sizes, traces, trace_offset, trace_owner, trace_cell, slowness, band_start, dip_shift):
    c = Sizes()
    size_x, c.nil = sizes
    c.nz = 1
    while c.nz * c.nz < size_x:
        c.nz *= 2
    c.nx = size_x // c.nz
    c.group = c.nx * c.nil
    count, c.samples = traces.shape
    c.cap = max(2, 5 * count // (4 * size_x * c.nil))
    c.rows = up_to(c.nz * c.cap, 16)
    c.meta_rows = up_to(c.rows, LANES)
    c.bx, c.by = slowness.shape[:2]
    c.batch = 2
    c.pieces = 3
    cells = c.bx * c.by
    bins = c.nz * cells
    samples = c.samples
    blocks = samples // LANES
    batch_rows = c.batch * c.rows
    lag_rows = up_to((c.bx + 2) * (c.by + 2), 8)
    dma = pltpu.SemaphoreType.DMA
    strip_count = 2 + 2 * c.bx + 4
    return pl.pallas_call(
        functools.partial(kernel, c),
        out_shape=jax.ShapeDtypeStruct((c.bx, c.by, samples), f32),
        in_specs=[pl.BlockSpec(memory_space=pltpu.VMEM)] * 3
        + [pl.BlockSpec(memory_space=pl.ANY)]
        + [pl.BlockSpec(memory_space=pltpu.VMEM)] * 2
        + [pl.BlockSpec(memory_space=pltpu.SMEM)],
        out_specs=pl.BlockSpec(memory_space=pltpu.VMEM),
        scratch_shapes=[
            pltpu.VMEM((count, samples), bf16),
            pltpu.VMEM((cells, samples), f32),
            pltpu.VMEM((1, samples), jnp.int32),
            pltpu.VMEM((c.group, c.rows, samples), bf16),
            pltpu.VMEM((c.group, 16, c.meta_rows), bf16),
            pltpu.VMEM((c.group * c.rows, samples + LANES), bf16),
            pltpu.VMEM((c.group, 16, c.meta_rows), bf16),
            pltpu.VMEM((c.nz, cells, samples), f32),
            pltpu.VMEM((4 * bins, samples), bf16),
            pltpu.VMEM((blocks, 2 * LANES, BAND * LANES), bf16),
            pltpu.VMEM((2, batch_rows, BAND * LANES), f32),
            pltpu.VMEM((2, batch_rows, LANES), f32),
            pltpu.VMEM((3, batch_rows, LANES), f32),
            pltpu.VMEM((c.nz, cells, samples + LANES), f32),
            pltpu.VMEM((c.nz - 1, cells, samples + LANES), f32),
            pltpu.VMEM(((c.bx + 2) * (c.by + 2), 1, samples), f32),
            pltpu.VMEM((up_to((2 * DIP + 1) * lag_rows, LANES), samples), f32),
            dma, dma((c.group,)), dma((c.group,)), dma((c.group,)), dma((c.group,)),
            dma((c.nz,)), dma((c.nz,)), dma((c.nz * c.pieces,)), dma((c.nz * c.pieces,)),
            dma((strip_count * c.pieces,)), dma((strip_count * c.pieces,)),
        ],
        compiler_params=pltpu.CompilerParams(
            collective_id=0, has_side_effects=True, vmem_limit_bytes=56 * 1024 * 1024
        ),
        name="bin_stack_smooth",
    )(trace_owner, trace_offset, trace_cell, traces, slowness, band_start, dip_shift.transpose(1, 2, 0))


def solution(mesh):
    sizes = (mesh.shape["xline"], mesh.shape["iline"])
    return jax.shard_map(
        functools.partial(body, sizes),
        mesh=mesh,
        in_specs=(
            P(("xline", "iline"), None),
            P(("xline", "iline")),
            P(("xline", "iline")),
            P(("xline", "iline")),
            P("xline", "iline", None),
            P(),
            P(None, "xline", "iline"),
        ),
        out_specs=P("xline", "iline", None),
        check_vma=False,
    )
```
